768 devices in a mesh: section: 96 (over z, x, core), ep: 8 (over y).
Axes of the slice: x: 4, y: 8, z: 12, core: 2. Of those that a mesh axis runs over, the one named last changes fastest.
Arguments:
- tokens: bfloat16 [2048, 1440], P('ep', 'section'), may hold values from -6 to 6
- grad_out: bfloat16 [2048, 1440], P('ep', 'section'), may hold values from -6 to 6
- expert_ids: int32 [2048, 4], P('ep'), may hold values from 0 to 7, all different within a row; in each aligned block of 256 rows (0 to 255, 256 to 511, ...) at most 192 rows name the same one
- probs: float32 [2048, 4], P('ep'), may hold values from 0.05 to 1
- w_gate: bfloat16 [8, 1440, 2880], P('ep', None, 'section'), may hold values from -0.15625 to 0.15625
- w_up: bfloat16 [8, 1440, 2880], P('ep', None, 'section'), may hold values from -0.15625 to 0.15625
- w_down: bfloat16 [8, 2880, 1440], P('ep', 'section'), may hold values from -0.109375 to 0.109375
Outputs:
- grad_gate: bfloat16 [8, 1440, 2880], P('ep', None, 'section')
- grad_up: bfloat16 [8, 1440, 2880], P('ep', None, 'section')
- grad_down: bfloat16 [8, 2880, 1440], P('ep', 'section')
The draws below stay inside these ranges and needn't reach their ends.
Inputs may be any that keep to these rules, and one draw needn't show every extreme that they name: `expert_ids`: among the picks of the 256 tokens of one index of ep, no expert is named more than 192 times, and the 4 experts of a token differ.
All inputs are finite; a program needn't handle non-finite values.
Results may differ from the reference program's by a relative error of at most 0.0065.
Values may be sent and summed in bfloat16 or wider, within the bound.
No kernel may reach another device: no remote copies, remote signals or barrier semaphores. Data moves between devices by JAX's collectives and lax.ppermute only.
A program may use at most 64 MiB of HBM per device.

```python
import math
import jax
import jax.numpy as jnp
import numpy as np
from jax import lax

D = 1440
FF = 2880
TOP = 4
TOK_DEV = 256
EXPERTS = 8
TOKENS = 2048
CAP = 192
N_EP = 8


def block_scale(stream_key, extent, shards, smallest, high):
    def one(position, parts):
        steps = jax.random.uniform(jax.random.fold_in(jax.random.fold_in(stream_key, 6), position), (parts,), jnp.float32, smallest / len(shards), high / len(shards))
        return jnp.repeat(jnp.exp(steps), extent[position] // parts).reshape((-1,) + (1,) * (len(extent) - position - 1))

    level = one(*shards[0])
    for cut in shards[1:]:
        level = level * one(*cut)
    return level


def shared_out(rng, own, number, rows, amount, top, most, slope):
    order = jax.random.permutation(rng, amount)
    heavy_load, usual = load_shares(amount, rows * top, most, slope, True), load_shares(amount, rows * top, most, slope, False)
    places = jnp.arange(amount)

    def named(tallies, turn):
        used = int((tallies > 0).sum())
        fixed = max(1, used // 4)
        shifted = fixed + (places - fixed + turn * (used - fixed)) % max(1, amount - fixed)
        return jnp.zeros((amount,), jnp.int32).at[order[jnp.where(places < fixed, places, shifted)]].set(jnp.asarray(tallies, jnp.int32))

    tallies = jnp.where(number % 4 == 0, named(heavy_load, number // 4), named(usual, number - number // 4 - 1))
    mixed = jax.random.permutation(jax.random.fold_in(own, 3), amount)
    giver, taker = mixed[0:amount // 2 * 2:2], mixed[1:amount // 2 * 2:2]
    room = jnp.minimum(tallies[giver] - 1, most - tallies[taker]) // 2
    room = jnp.where((giver == order[0]) | (taker == order[0]) | (tallies[taker] == 0), 0, jnp.maximum(room, 0))
    shifted = jax.random.randint(jax.random.fold_in(own, 4), (amount // 2,), 0, 1 << 20) % (room + 1)
    tallies = tallies.at[giver].add(-shifted).at[taker].add(shifted)
    labels = jnp.searchsorted(jnp.cumsum(tallies), jnp.arange(rows * top), side="right").astype(jnp.int32)
    listing = labels.reshape(top, rows).T
    listing = listing[jax.random.permutation(jax.random.fold_in(own, 1), rows)]
    turn = jax.random.randint(jax.random.fold_in(own, 2), (rows, 1), 0, top)
    return jnp.take_along_axis(listing, (jnp.arange(top)[None, :] + turn) % top, axis=1)


def load_shares(count, total, most, lean, full):
    loads = [(1 << 20) // math.isqrt(standing ** lean) + 1 for standing in range(1, count + 1)]
    largest = most if full else min(most, max(-(-total // count), total * loads[0] // sum(loads)))
    least = 1 if total - largest >= count - 1 else 0
    holding, surplus = [largest] + [least] * (count - 1), total - largest - least * (count - 1)
    while surplus > 0:
        movable = [i for i in range(1, count) if holding[i] < largest] or [i for i in range(1, count) if holding[i] < most]
        mass, remaining = sum([loads[i] for i in movable]), surplus
        for i in movable:
            extra = min(most - holding[i], max(1, remaining * loads[i] // mass), surplus)
            holding[i] = holding[i] + extra
            surplus = surplus - extra
    return np.array(holding)


def noise(own_key, extent, deviation, reach, split=(), kind=jnp.bfloat16):
    array = jax.random.normal(own_key, extent, jnp.float32) * deviation
    if len(split) > 0:
        array = block_scale(own_key, extent, split, -0.22, 0.18) * array
    return jnp.clip(array, min=-reach, max=reach).astype(kind)


def setup_inputs(seed: int = 0) -> dict:
    keys = jax.random.split(jax.random.key(seed), 8)
    tokens = noise(keys[0], (TOKENS, D), 1.0, 6.0, ((0, 8), (1, 96)))
    grad_out = noise(keys[1], (TOKENS, D), 1.0, 6.0, ((0, 8), (1, 96)))
    expert_ids_keys = jax.random.split(jax.random.fold_in(keys[2], 1), TOKENS // TOK_DEV)
    expert_ids_turns = jax.random.permutation(jax.random.fold_in(keys[2], 3), TOKENS // TOK_DEV)
    expert_ids = jax.vmap(lambda own, number: shared_out(jax.random.fold_in(keys[2], 2), own, number, TOK_DEV, EXPERTS, TOP, CAP, 2))(expert_ids_keys, expert_ids_turns).reshape((TOKENS, TOP))
    probs = jnp.clip(jnp.exp(math.log(1.0) - 2.9957323 * jax.random.uniform(keys[3], (TOKENS, TOP), jnp.float32) ** block_scale(keys[3], (TOKENS, TOP), ((0, 8),), -0.2, 0.2)), 0.05, 1.0)
    w_gate = noise(keys[4], (EXPERTS, D, FF), D ** -0.5, 0.15625, ((0, 8), (2, 96)))
    w_up = noise(keys[5], (EXPERTS, D, FF), D ** -0.5, 0.15625, ((0, 8), (2, 96)))
    w_down = noise(keys[6], (EXPERTS, FF, D), FF ** -0.5, 0.109375, ((0, 8), (1, 96)))
    return {"tokens": tokens, "grad_out": grad_out, "expert_ids": expert_ids, "probs": probs, "w_gate": w_gate, "w_up": w_up, "w_down": w_down}


def rounded(value):
    return lax.optimization_barrier(value.astype(jnp.bfloat16)).astype(jnp.float32)


def reference(tokens, grad_out, expert_ids, probs, w_gate, w_up, w_down):
    picks = TOKENS * TOP
    flat_ids = expert_ids.reshape(picks).astype(jnp.int32)
    flat_probs = probs.reshape(picks)
    order = jnp.argsort(flat_ids, stable=True).astype(jnp.int32)
    counts = jnp.sum((flat_ids[:, None] == jnp.arange(EXPERTS, dtype=jnp.int32)[None, :]).astype(jnp.int32), axis=0)
    starts = (jnp.cumsum(counts) - counts).astype(jnp.int32)
    most_rows = N_EP * CAP
    slot_rows = jnp.arange(most_rows, dtype=jnp.int32)

    def one_expert(items):
        expert, gate_w, up_w, down_w = items
        start = starts[expert]
        count = counts[expert]
        where_pick = order[jnp.clip(start + slot_rows, 0, picks - 1)]
        valid = slot_rows < count
        token_row = (where_pick // TOP).astype(jnp.int32)
        inputs = tokens[token_row] * valid[:, None].astype(jnp.bfloat16)
        weight = jnp.where(valid, flat_probs[where_pick], 0.0)
        scaled = (weight[:, None] * grad_out[token_row].astype(jnp.float32)).astype(jnp.bfloat16)
        gate = jnp.dot(inputs, gate_w, preferred_element_type=jnp.float32)
        linear = jnp.dot(inputs, up_w, preferred_element_type=jnp.float32)
        sigma = jax.nn.sigmoid(gate)
        hidden = (gate * sigma * linear).astype(jnp.bfloat16)
        grad_hidden = jnp.dot(scaled, down_w.T, preferred_element_type=jnp.float32)
        gate_term = (grad_hidden * linear * sigma * (1.0 + gate * (1.0 - sigma))).astype(jnp.bfloat16)
        linear_term = (grad_hidden * gate * sigma).astype(jnp.bfloat16)
        lower = valid & (token_row < TOKENS // 2)
        upper = valid & (token_row >= TOKENS // 2)
        totals = []
        for mask in (lower, upper):
            weight_mask = mask[:, None].astype(jnp.bfloat16)
            masked_in = inputs * weight_mask
            masked_hidden = hidden * weight_mask
            part_gate = rounded(jnp.dot(masked_in.T, gate_term, preferred_element_type=jnp.float32))
            part_up = rounded(jnp.dot(masked_in.T, linear_term, preferred_element_type=jnp.float32))
            part_down = rounded(jnp.dot(masked_hidden.T, scaled, preferred_element_type=jnp.float32))
            totals.append((part_gate, part_up, part_down))
        return ((totals[0][0] + totals[1][0]).astype(jnp.bfloat16),
                (totals[0][1] + totals[1][1]).astype(jnp.bfloat16),
                (totals[0][2] + totals[1][2]).astype(jnp.bfloat16))

    grad_gate, grad_up, grad_down = lax.map(one_expert, (jnp.arange(EXPERTS, dtype=jnp.int32), w_gate, w_up, w_down))
    return grad_gate, grad_up, grad_down
```

```python
import functools

import jax
import jax.numpy as jnp
from jax import lax
from jax.experimental import pallas as pl
from jax.experimental.pallas import tpu as pltpu
from jax.sharding import Mesh, PartitionSpec as P

BF16, F32 = jnp.bfloat16, jnp.float32
CORES = 2
CHIPS_X = 4
PAIR = 2
LANES = 128
SEC = ("z", "x", "core")
EP = ("yo", "yi")


def dot(a, b):
    return jnp.dot(a, b, preferred_element_type=F32)


def dot_t(a, b):
    return lax.dot_general(a, b, (((1,), (1,)), ((), ())), preferred_element_type=F32)


def spread(narrow_lane, wide_lane):
    return (narrow_lane == wide_lane - (wide_lane >> 4)) & ((wide_lane & 15) != 15)


def widen(rows, wide):
    narrow = rows.shape[1]
    pieces = []
    for start in range(0, wide, LANES):
        low = start - start // 16
        low = low // LANES * LANES
        high = min(narrow, low + 2 * LANES)
        source = lax.broadcasted_iota(jnp.int32, (high - low, LANES), 0) + low
        target = lax.broadcasted_iota(jnp.int32, (high - low, LANES), 1) + start
        chosen = spread(source, target).astype(F32).astype(BF16)
        pieces.append(dot(rows[:, low:high], chosen).astype(BF16))
    return jnp.concatenate(pieces, axis=1)


def narrowed(rows, narrow):
    wide = rows.shape[1]
    pieces = []
    for start in range(0, narrow, LANES):
        width = min(LANES, narrow - start)
        low = start // 15 * 16 // LANES * LANES
        last = start + width - 1
        high = min(wide, -(-(last // 15 * 16 + last % 15 + 1) // LANES) * LANES)
        source = lax.broadcasted_iota(jnp.int32, (high - low, width), 0) + low
        target = lax.broadcasted_iota(jnp.int32, (high - low, width), 1) + start
        chosen = spread(target, source).astype(F32).astype(BF16)
        pieces.append(dot(rows[:, low:high], chosen).astype(BF16))
    return jnp.concatenate(pieces, axis=1)


def pack_kernel(place, tokens, cotangent, ids, probs, out):
    width, count = tokens.shape
    mine = ids[...] == place[0]
    weight = jnp.sum(jnp.where(mine, probs[...], 0.0), axis=0, keepdims=True)
    high = weight.astype(BF16).astype(F32)
    low = weight - high
    left = jnp.concatenate([tokens[...].astype(F32), high], axis=0)
    right = jnp.concatenate([cotangent[...].astype(F32), low], axis=0)
    out[:, :count] = left.astype(BF16)
    out[:, count:] = right.astype(BF16)


def weights_kernel(gate_w, up_w, down_w, out):
    hidden, wide = out.shape[0] // 3, out.shape[1]
    units = gate_w.shape[0]
    filler = jnp.zeros((hidden - units, gate_w.shape[1]), F32)
    rows = []
    for ref in (gate_w, up_w, down_w):
        rows += [ref[...].astype(F32), filler]
    out[...] = widen(jnp.concatenate(rows, axis=0).astype(BF16), wide)


def grads_kernel(place, own, other, weights, out, inputs, cotangents, sems):
    chips_x, chips_z, pair, depth, both = own.shape
    count = both // 2
    groups, stacked, wide = weights.shape
    hidden = stacked // 3
    core, yi = place[0], place[1]
    copies = []
    for s, ref in enumerate((own, other)):
        slot = core if s == 0 else 1 - core
        for x in range(chips_x):
            for y in range(pair):
                for k, held in enumerate((inputs, cotangents)):
                    copies.append(
                        pltpu.make_async_copy(
                            ref.at[x, :, y, :, pl.ds(k * count, count)],
                            held.at[:, x * CORES + slot, :, pl.ds(y * count, count)],
                            sems.at[s, x, y, k],
                        )
                    )
    for copy in copies:
        copy.start()
    for copy in copies:
        copy.wait()
    total = pair * count
    rows = inputs[...].reshape(wide, total)
    backs = cotangents[...].reshape(wide, total)

    def part(k):
        return weights[:, k * hidden : (k + 1) * hidden, :].reshape(groups * hidden, wide)

    gate = dot(part(0), rows)
    linear = dot(part(1), rows)
    back = dot(part(2), backs)
    shares = []
    for j in range(groups):
        high = inputs[j * PAIR + yi, 0].astype(F32)[depth - 1 : depth]
        low = cotangents[j * PAIR + yi, 0].astype(F32)[depth - 1 : depth]
        shares.append(jnp.broadcast_to(high + low, (hidden, total)))
    share = jnp.concatenate(shares, axis=0)
    back = back * share
    sigma = jax.nn.sigmoid(gate)
    lifted = (gate * sigma * linear * share).astype(BF16)
    gate_term = (back * linear * sigma * (1.0 + gate * (1.0 - sigma))).astype(BF16)
    linear_term = (back * gate * sigma).astype(BF16)
    for k, (left, right) in enumerate(((gate_term, rows), (linear_term, rows), (lifted, backs))):
        grad = dot_t(left, right).astype(BF16)
        out[:, k * hidden : (k + 1) * hidden, :] = grad.reshape(groups, hidden, wide)


def total_kernel(parts, gate_g, up_g, down_g):
    hidden = parts.shape[1] // 3
    total = parts[0].astype(F32)
    for j in range(1, parts.shape[0]):
        total = total + parts[j].astype(F32)
    units, narrow = gate_g.shape
    slim = narrowed(total.astype(BF16), narrow).astype(F32)
    for k, ref in enumerate((gate_g, up_g, down_g)):
        ref[...] = slim[k * hidden : k * hidden + units].astype(BF16)


VMEM = pl.BlockSpec(memory_space=pltpu.VMEM)
SMEM = pl.BlockSpec(memory_space=pltpu.SMEM)
ANY = pl.BlockSpec(memory_space=pl.ANY)
PARAMS = pltpu.CompilerParams(vmem_limit_bytes=40 * 1024 * 1024)


def swap(value, axis):
    return lax.ppermute(value, axis, [(0, 1), (1, 0)])


def shards(tokens, grad_out, expert_ids, probs, w_gate, w_up, w_down):
    chips_z, chips_x, groups = lax.axis_size("z"), lax.axis_size("x"), lax.axis_size("yo")
    count, width = tokens.shape
    features, units = w_gate.shape[1:]
    depth = width + 1
    wide = chips_z * chips_x * CORES * depth
    hidden = -(-units // 16) * 16
    core, yi = lax.axis_index("core"), lax.axis_index("yi")

    packed = pl.pallas_call(
        pack_kernel,
        out_shape=jax.ShapeDtypeStruct((depth, 2 * count), BF16),
        in_specs=[SMEM, VMEM, VMEM, VMEM, VMEM],
        out_specs=VMEM,
        name="pack",
    )(lax.axis_index("z").reshape(1), tokens.T, grad_out.T, expert_ids.T, probs.T)
    paired = jnp.stack([packed, swap(packed, "yi")])
    along_z = lax.all_gather(paired, "z")
    along_x = lax.all_to_all(
        jnp.broadcast_to(along_z[None], (chips_x,) + along_z.shape), "x", split_axis=0, concat_axis=0, tiled=True
    )
    crossed = swap(along_x, "core")

    stacked = pl.pallas_call(
        weights_kernel,
        out_shape=jax.ShapeDtypeStruct((3 * hidden, wide), BF16),
        in_specs=[VMEM] * 3,
        out_specs=VMEM,
        name="widen_weights",
    )(w_gate[0].T, w_up[0].T, w_down[0])
    weights = lax.all_gather(stacked, "yo")

    parts = pl.pallas_call(
        grads_kernel,
        out_shape=jax.ShapeDtypeStruct((groups, 3 * hidden, wide), BF16),
        in_specs=[SMEM, ANY, ANY, VMEM],
        out_specs=VMEM,
        scratch_shapes=[
            pltpu.VMEM((chips_z, chips_x * CORES, depth, PAIR * count), BF16),
            pltpu.VMEM((chips_z, chips_x * CORES, depth, PAIR * count), BF16),
            pltpu.SemaphoreType.DMA((2, chips_x, PAIR, 2)),
        ],
        compiler_params=PARAMS,
        name="grads",
    )(jnp.stack([core, yi]), along_x, crossed, weights)
    met = lax.all_to_all(parts, "yo", split_axis=0, concat_axis=0, tiled=True)
    grad_gate, grad_up, grad_down = pl.pallas_call(
        total_kernel,
        out_shape=[jax.ShapeDtypeStruct((units, features), BF16)] * 3,
        in_specs=[VMEM],
        out_specs=[VMEM] * 3,
        name="total",
    )(met)
    return grad_gate.T[None], grad_up.T[None], grad_down[None]


def solution(mesh, chips_x=CHIPS_X):
    section, ep = mesh.devices.shape
    shape = (section // (chips_x * CORES), chips_x, CORES, ep // PAIR, PAIR)
    fine = Mesh(mesh.devices.reshape(shape), SEC + EP)
    placed = (
        P(EP, SEC),
        P(EP, SEC),
        P(EP, None),
        P(EP, None),
        P(EP, None, SEC),
        P(EP, None, SEC),
        P(EP, SEC, None),
    )
    return jax.shard_map(
        shards,
        mesh=fine,
        in_specs=placed,
        out_specs=(P(EP, None, SEC), P(EP, None, SEC), P(EP, SEC, None)),
        check_vma=False,
    )
```

```python
import functools

import jax
import jax.numpy as jnp
from jax import lax
from jax.experimental import pallas as pl
from jax.experimental.pallas import tpu as pltpu
from jax.sharding import Mesh, PartitionSpec as P

BF16, F32 = jnp.bfloat16, jnp.float32
CORES = 2
CHIPS_X = 4
PAIR = 2
LANES = 128
SEC = ("zo", "zi", "x", "core")
EP = ("yo", "yi")
GROUP = ("zi", "yi")


def dot(a, b):
    return jnp.dot(a, b, preferred_element_type=F32)


def dot_t(a, b):
    return lax.dot_general(a, b, (((1,), (1,)), ((), ())), preferred_element_type=F32)


def spread(narrow_lane, wide_lane):
    return (narrow_lane == wide_lane - (wide_lane >> 4)) & ((wide_lane & 15) != 15)


def widen(rows, wide):
    narrow = rows.shape[1]
    pieces = []
    for start in range(0, wide, LANES):
        low = start - start // 16
        low = low // LANES * LANES
        high = min(narrow, low + 2 * LANES)
        source = lax.broadcasted_iota(jnp.int32, (high - low, LANES), 0) + low
        target = lax.broadcasted_iota(jnp.int32, (high - low, LANES), 1) + start
        chosen = spread(source, target).astype(F32).astype(BF16)
        pieces.append(dot(rows[:, low:high], chosen).astype(BF16))
    return jnp.concatenate(pieces, axis=1)


def narrowed(rows, narrow):
    wide = rows.shape[1]
    pieces = []
    for start in range(0, narrow, LANES):
        width = min(LANES, narrow - start)
        low = start // 15 * 16 // LANES * LANES
        last = start + width - 1
        high = min(wide, -(-(last // 15 * 16 + last % 15 + 1) // LANES) * LANES)
        source = lax.broadcasted_iota(jnp.int32, (high - low, width), 0) + low
        target = lax.broadcasted_iota(jnp.int32, (high - low, width), 1) + start
        chosen = spread(target, source).astype(F32).astype(BF16)
        pieces.append(dot(rows[:, low:high], chosen).astype(BF16))
    return jnp.concatenate(pieces, axis=1)


def half_turn(tile):
    return pltpu.roll(tile, LANES // 2, 1)


def turned(rows):
    tiles = [half_turn(rows[:, k : k + LANES]) for k in range(0, rows.shape[1], LANES)]
    return jnp.concatenate(tiles, axis=1)


def pack_kernel(place, tokens, cotangent, ids, probs, out):
    count = tokens.shape[1]
    mine = ids[...] == place[0]
    weight = jnp.sum(jnp.where(mine, probs[...], 0.0), axis=0, keepdims=True)
    high = weight.astype(BF16).astype(F32)
    left = jnp.concatenate([tokens[...].astype(F32), high], axis=0)
    right = jnp.concatenate([cotangent[...].astype(F32), weight - high], axis=0)
    odd = place[1] == 1
    first, second = jnp.where(odd, right, left), jnp.where(odd, left, right)
    lower = lax.broadcasted_iota(jnp.int32, (first.shape[0], LANES), 1) < LANES // 2
    for tile in range(count // LANES):
        a, b = first[:, tile * LANES : (tile + 1) * LANES], second[:, tile * LANES : (tile + 1) * LANES]
        quarters = (jnp.where(lower, a, half_turn(b)), jnp.where(lower, half_turn(a), b))
        for k, quarter in enumerate(quarters):
            zi, yi = divmod(2 * tile + k, PAIR)
            for yo in range(out.shape[1]):
                out[zi, yo, yi] = quarter.astype(BF16)


def weights_kernel(gate_w, up_w, down_w, out):
    hidden, wide = out.shape[0] // 3, out.shape[1]
    units = gate_w.shape[0]
    filler = jnp.zeros((hidden - units, gate_w.shape[1]), F32)
    rows = []
    for ref in (gate_w, up_w, down_w):
        rows += [ref[...].astype(F32), filler]
    out[...] = widen(jnp.concatenate(rows, axis=0).astype(BF16), wide)


def grads_kernel(place, own, other, weights, out, inputs, cotangents, near, sems):
    chips_x, chips_z, blocks, depth, lanes = own.shape
    groups, stacked, wide = weights.shape
    hidden = stacked // 3
    core, yo = place[0], place[1]
    lower = lax.broadcasted_iota(jnp.int32, (chips_z, depth, lanes), 2) < lanes // 2
    copies = [pltpu.make_async_copy(own.at[x], near.at[x], sems.at[x]) for x in range(chips_x)]
    for copy in copies:
        copy.start()
    for ref, slot in ((other, 1 - core), (near, core)):
        for x in range(chips_x):
            if ref is near:
                copies[x].wait()
            for pair in range(blocks // 2):
                even, odd = ref[x, :, 2 * pair], ref[x, :, 2 * pair + 1]
                at = slice(pair * lanes, (pair + 1) * lanes)
                inputs[:, x * CORES + slot, :, at] = jnp.where(lower, even, odd)
                cotangents[:, x * CORES + slot, :, at] = jnp.where(lower, odd, even)
    total = blocks // 2 * lanes
    rows = inputs[...].reshape(wide, total)
    backs = cotangents[...].reshape(wide, total)

    def part(k):
        return weights[:, k * hidden : (k + 1) * hidden, :].reshape(groups * hidden, wide)

    gate = dot(part(0), rows)
    linear = dot(part(1), rows)
    back = turned(dot(part(2), backs))
    shares = []
    for j in range(groups):
        expert = yo * PAIR + j % PAIR
        high = inputs[expert, 0].astype(F32)[depth - 1 : depth]
        low = turned(cotangents[expert, 0].astype(F32))[depth - 1 : depth]
        shares.append(jnp.broadcast_to(high + low, (hidden, total)))
    share = jnp.concatenate(shares, axis=0)
    back = back * share
    sigma = jax.nn.sigmoid(gate)
    lifted = turned(gate * sigma * linear * share).astype(BF16)
    gate_term = (back * linear * sigma * (1.0 + gate * (1.0 - sigma))).astype(BF16)
    linear_term = (back * gate * sigma).astype(BF16)
    for k, (left, right) in enumerate(((gate_term, rows), (linear_term, rows), (lifted, backs))):
        grad = dot_t(left, right).astype(BF16)
        out[:, k * hidden : (k + 1) * hidden, :] = grad.reshape(groups, hidden, wide)


def total_kernel(parts, gate_g, up_g, down_g):
    hidden = parts.shape[1] // 3
    total = parts[0].astype(F32)
    for j in range(1, parts.shape[0]):
        total = total + parts[j].astype(F32)
    units, narrow = gate_g.shape
    slim = narrowed(total.astype(BF16), narrow).astype(F32)
    for k, ref in enumerate((gate_g, up_g, down_g)):
        ref[...] = slim[k * hidden : k * hidden + units].astype(BF16)


VMEM = pl.BlockSpec(memory_space=pltpu.VMEM)
SMEM = pl.BlockSpec(memory_space=pltpu.SMEM)
ANY = pl.BlockSpec(memory_space=pl.ANY)
PARAMS = pltpu.CompilerParams(vmem_limit_bytes=40 * 1024 * 1024)


def after(value, earlier):
    return pl.pallas_call(
        lambda value_ref, earlier_ref, out_ref: None,
        out_shape=jax.ShapeDtypeStruct(value.shape, value.dtype),
        in_specs=[ANY, ANY],
        out_specs=ANY,
        input_output_aliases={0: 0},
        name="after",
    )(value, earlier)


def swap(value, axis):
    return lax.ppermute(value, axis, [(0, 1), (1, 0)])


def shards(tokens, grad_out, expert_ids, probs, w_gate, w_up, w_down):
    pairs_z, chips_x, pairs_y = lax.axis_size("zo"), lax.axis_size("x"), lax.axis_size("yo")
    chips_z, groups = pairs_z * PAIR, PAIR * PAIR
    count, width = tokens.shape
    features, units = w_gate.shape[1:]
    depth = width + 1
    wide = chips_z * chips_x * CORES * depth
    hidden = -(-units // 16) * 16
    zone = lax.axis_index(("zo", "zi"))

    packed = pl.pallas_call(
        pack_kernel,
        out_shape=jax.ShapeDtypeStruct((PAIR, pairs_y, PAIR, depth, LANES), BF16),
        in_specs=[SMEM, VMEM, VMEM, VMEM, VMEM],
        out_specs=VMEM,
        name="pack",
    )(jnp.stack([zone, lax.axis_index("yi")]), tokens.T, grad_out.T, expert_ids.T, probs.T)
    stacked = pl.pallas_call(
        weights_kernel,
        out_shape=jax.ShapeDtypeStruct((3 * hidden, wide), BF16),
        in_specs=[VMEM] * 3,
        out_specs=VMEM,
        name="widen_weights",
    )(w_gate[0].T, w_up[0].T, w_down[0])
    sent = packed.reshape(PAIR * pairs_y * PAIR, depth, LANES)
    quarter = lax.all_to_all(sent, ("zi",) + EP, split_axis=0, concat_axis=0, tiled=True)
    quarter, stacked = lax.optimization_barrier((quarter, stacked))
    weights = lax.all_gather(stacked, GROUP)
    along_z = lax.all_gather(quarter, "zo").reshape(chips_z, pairs_y * PAIR, depth, LANES)
    along_x = lax.all_to_all(
        jnp.broadcast_to(along_z[None], (chips_x,) + along_z.shape), "x", split_axis=0, concat_axis=0, tiled=True
    )
    along_x = after(along_x, weights)
    crossed = swap(along_x, "core")

    tokens_held = pairs_y * LANES
    parts = pl.pallas_call(
        grads_kernel,
        out_shape=jax.ShapeDtypeStruct((groups, 3 * hidden, wide), BF16),
        in_specs=[SMEM, ANY, VMEM, VMEM],
        out_specs=VMEM,
        scratch_shapes=[pltpu.VMEM((chips_z, chips_x * CORES, depth, tokens_held), BF16)] * 2
        + [pltpu.VMEM(along_x.shape, BF16), pltpu.SemaphoreType.DMA((chips_x,))],
        compiler_params=PARAMS,
        name="grads",
    )(jnp.stack([lax.axis_index("core"), lax.axis_index("yo")]), along_x, crossed, weights)
    met = lax.all_to_all(parts, GROUP, split_axis=0, concat_axis=0, tiled=True)
    grad_gate, grad_up, grad_down = pl.pallas_call(
        total_kernel,
        out_shape=[jax.ShapeDtypeStruct((units, features), BF16)] * 3,
        in_specs=[VMEM],
        out_specs=[VMEM] * 3,
        name="total",
    )(met)
    return grad_gate.T[None], grad_up.T[None], grad_down[None]


def solution(mesh, chips_x=CHIPS_X):
    section, ep = mesh.devices.shape
    shape = (section // (chips_x * CORES * PAIR), PAIR, chips_x, CORES, ep // PAIR, PAIR)
    fine = Mesh(mesh.devices.reshape(shape), SEC + EP)
    placed = (
        P(EP, SEC),
        P(EP, SEC),
        P(EP, None),
        P(EP, None),
        P(EP, None, SEC),
        P(EP, None, SEC),
        P(EP, SEC, None),
    )
    return jax.shard_map(
        shards,
        mesh=fine,
        in_specs=placed,
        out_specs=(P(EP, None, SEC), P(EP, None, SEC), P(EP, SEC, None)),
        check_vma=False,
    )
```

```python
import functools

import jax
import jax.numpy as jnp
from jax import lax
from jax.experimental import pallas as pl
from jax.experimental.pallas import tpu as pltpu
from jax.sharding import Mesh, PartitionSpec as P

BF16, F32 = jnp.bfloat16, jnp.float32
CORES = 2
CHIPS_X = 4
PAIR = 2
LANES = 128
SEC = ("zo", "zi", "x", "core")
EP = ("yo", "yi")
GROUP = ("zi", "yi")


def dot(a, b):
    return jnp.dot(a, b, preferred_element_type=F32)


def dot_t(a, b):
    return lax.dot_general(a, b, (((1,), (1,)), ((), ())), preferred_element_type=F32)


def spread(narrow_lane, wide_lane):
    return (narrow_lane == wide_lane - (wide_lane >> 4)) & ((wide_lane & 15) != 15)


def widen(rows, wide):
    narrow = rows.shape[1]
    pieces = []
    for start in range(0, wide, LANES):
        low = start - start // 16
        low = low // LANES * LANES
        high = min(narrow, low + 2 * LANES)
        source = lax.broadcasted_iota(jnp.int32, (high - low, LANES), 0) + low
        target = lax.broadcasted_iota(jnp.int32, (high - low, LANES), 1) + start
        chosen = spread(source, target).astype(F32).astype(BF16)
        pieces.append(dot(rows[:, low:high], chosen).astype(BF16))
    return jnp.concatenate(pieces, axis=1)


def narrowed(rows, narrow):
    wide = rows.shape[1]
    pieces = []
    for start in range(0, narrow, LANES):
        width = min(LANES, narrow - start)
        low = start // 15 * 16 // LANES * LANES
        last = start + width - 1
        high = min(wide, -(-(last // 15 * 16 + last % 15 + 1) // LANES) * LANES)
        source = lax.broadcasted_iota(jnp.int32, (high - low, width), 0) + low
        target = lax.broadcasted_iota(jnp.int32, (high - low, width), 1) + start
        chosen = spread(target, source).astype(F32).astype(BF16)
        pieces.append(dot(rows[:, low:high], chosen).astype(BF16))
    return jnp.concatenate(pieces, axis=1)


def half_turn(tile):
    return pltpu.roll(tile, LANES // 2, 1)


def turned(rows):
    tiles = [half_turn(rows[:, k : k + LANES]) for k in range(0, rows.shape[1], LANES)]
    return jnp.concatenate(tiles, axis=1)


def pack_kernel(zone, yi, tokens, cotangent, ids, probs, out):
    count = tokens.shape[1]
    mine = ids[...] == zone[0]
    weight = jnp.sum(jnp.where(mine, probs[...], 0.0), axis=0, keepdims=True)
    high = weight.astype(BF16).astype(F32)
    left = jnp.concatenate([tokens[...].astype(F32), high], axis=0)
    right = jnp.concatenate([cotangent[...].astype(F32), weight - high], axis=0)
    odd = yi[0] == 1
    first, second = jnp.where(odd, right, left), jnp.where(odd, left, right)
    lower = lax.broadcasted_iota(jnp.int32, (first.shape[0], LANES), 1) < LANES // 2
    for tile in range(count // LANES):
        a, b = first[:, tile * LANES : (tile + 1) * LANES], second[:, tile * LANES : (tile + 1) * LANES]
        quarters = (jnp.where(lower, a, half_turn(b)), jnp.where(lower, half_turn(a), b))
        for k, quarter in enumerate(quarters):
            zi, yi = divmod(2 * tile + k, PAIR)
            for yo in range(out.shape[1]):
                out[zi, yo, yi] = quarter.astype(BF16)


def weights_kernel(gate_w, up_w, down_w, out):
    hidden, wide = out.shape[0] // 3, out.shape[1]
    units = gate_w.shape[0]
    filler = jnp.zeros((hidden - units, gate_w.shape[1]), F32)
    rows = []
    for ref in (gate_w, up_w, down_w):
        rows += [ref[...].astype(F32), filler]
    out[...] = widen(jnp.concatenate(rows, axis=0).astype(BF16), wide)


def grads_kernel(core_at, yo_at, own, other, gathered, out, inputs, cotangents, held, weights, sems, weights_sem):
    chips_x, chips_z, blocks, depth, lanes = own.shape
    groups, stacked, wide = weights.shape
    hidden = stacked // 3
    core, yo = core_at[0], yo_at[0]
    lower = lax.broadcasted_iota(jnp.int32, (chips_z, depth, lanes), 2) < lanes // 2
    copies = [
        [pltpu.make_async_copy(ref.at[x], held.at[s, x], sems.at[s, x]) for x in range(chips_x)]
        for s, ref in enumerate((own, other))
    ]
    weights_copy = pltpu.make_async_copy(gathered, weights, weights_sem)
    for copy in copies[0] + copies[1] + [weights_copy]:
        copy.start()
    for s, slot in ((0, core), (1, 1 - core)):
        for x in range(chips_x):
            copies[s][x].wait()
            for pair in range(blocks // 2):
                even, odd = held[s, x, :, 2 * pair], held[s, x, :, 2 * pair + 1]
                at = slice(pair * lanes, (pair + 1) * lanes)
                inputs[:, x * CORES + slot, :, at] = jnp.where(lower, even, odd)
                cotangents[:, x * CORES + slot, :, at] = jnp.where(lower, odd, even)
    weights_copy.wait()
    total = blocks // 2 * lanes
    rows = inputs[...].reshape(wide, total)
    backs = cotangents[...].reshape(wide, total)

    def part(k):
        return weights[:, k * hidden : (k + 1) * hidden, :].reshape(groups * hidden, wide)

    gate = dot(part(0), rows)
    linear = dot(part(1), rows)
    back = turned(dot(part(2), backs))
    shares = []
    for j in range(groups):
        expert = yo * PAIR + j % PAIR
        high = inputs[expert, 0].astype(F32)[depth - 1 : depth]
        low = turned(cotangents[expert, 0].astype(F32))[depth - 1 : depth]
        shares.append(jnp.broadcast_to(high + low, (hidden, total)))
    share = jnp.concatenate(shares, axis=0)
    back = back * share
    sigma = jax.nn.sigmoid(gate)
    lifted = turned(gate * sigma * linear * share).astype(BF16)
    gate_term = (back * linear * sigma * (1.0 + gate * (1.0 - sigma))).astype(BF16)
    linear_term = (back * gate * sigma).astype(BF16)
    for k, (left, right) in enumerate(((gate_term, rows), (linear_term, rows), (lifted, backs))):
        grad = dot_t(left, right).astype(BF16)
        out[:, k * hidden : (k + 1) * hidden, :] = grad.reshape(groups, hidden, wide)


def total_kernel(parts, gate_g, up_g, down_g):
    hidden = parts.shape[1] // 3
    total = parts[0].astype(F32)
    for j in range(1, parts.shape[0]):
        total = total + parts[j].astype(F32)
    units, narrow = gate_g.shape
    slim = narrowed(total.astype(BF16), narrow).astype(F32)
    for k, ref in enumerate((gate_g, up_g, down_g)):
        ref[...] = slim[k * hidden : k * hidden + units].astype(BF16)


VMEM = pl.BlockSpec(memory_space=pltpu.VMEM)
SMEM = pl.BlockSpec(memory_space=pltpu.SMEM)
ANY = pl.BlockSpec(memory_space=pl.ANY)
HBM = pl.BlockSpec(memory_space=pltpu.HBM)


def room(mib):
    return pltpu.CompilerParams(vmem_limit_bytes=mib * 1024 * 1024)


def after(value, earlier):
    return pl.pallas_call(
        lambda value_ref, earlier_ref, out_ref: None,
        out_shape=jax.ShapeDtypeStruct(value.shape, value.dtype),
        in_specs=[ANY, ANY],
        out_specs=ANY,
        input_output_aliases={0: 0},
        compiler_params=room(1),
        name="after",
    )(value, earlier)


def swap(value, axis):
    return lax.ppermute(value, axis, [(0, 1), (1, 0)])


def shards(tokens, grad_out, expert_ids, probs, w_gate, w_up, w_down):
    pairs_z, chips_x, pairs_y = lax.axis_size("zo"), lax.axis_size("x"), lax.axis_size("yo")
    chips_z, groups = pairs_z * PAIR, PAIR * PAIR
    count, width = tokens.shape
    features, units = w_gate.shape[1:]
    depth = width + 1
    wide = chips_z * chips_x * CORES * depth
    hidden = -(-units // 16) * 16
    zone = lax.axis_index(("zo", "zi"))

    packed = pl.pallas_call(
        pack_kernel,
        out_shape=jax.ShapeDtypeStruct((PAIR, pairs_y, PAIR, depth, LANES), BF16),
        in_specs=[SMEM, SMEM, VMEM, VMEM, VMEM, VMEM],
        out_specs=VMEM,
        name="pack",
    )(zone.reshape(1), lax.axis_index("yi").reshape(1), tokens.T, grad_out.T, expert_ids.T, probs.T)
    stacked = pl.pallas_call(
        weights_kernel,
        out_shape=jax.ShapeDtypeStruct((3 * hidden, wide), BF16),
        in_specs=[VMEM] * 3,
        out_specs=VMEM,
        name="widen_weights",
    )(w_gate[0].T, w_up[0].T, w_down[0])
    sent = packed.reshape(PAIR * pairs_y * PAIR, depth, LANES)
    quarter = lax.all_to_all(sent, ("zi",) + EP, split_axis=0, concat_axis=0, tiled=True)
    quarter, stacked = lax.optimization_barrier((quarter, stacked))
    weights = lax.all_gather(stacked, GROUP)
    along_z = lax.all_gather(quarter, "zo").reshape(chips_z, pairs_y * PAIR, depth, LANES)
    along_x = lax.all_to_all(
        jnp.broadcast_to(along_z[None], (chips_x,) + along_z.shape), "x", split_axis=0, concat_axis=0, tiled=True
    )
    along_x = after(along_x, weights[0, :16, :LANES])
    crossed = swap(along_x, "core")

    tokens_held = pairs_y * LANES
    parts = pl.pallas_call(
        grads_kernel,
        out_shape=jax.ShapeDtypeStruct((groups, 3 * hidden, wide), BF16),
        in_specs=[SMEM, SMEM, ANY, ANY, HBM],
        out_specs=VMEM,
        scratch_shapes=[pltpu.VMEM((chips_z, chips_x * CORES, depth, tokens_held), BF16)] * 2
        + [pltpu.VMEM((2,) + along_x.shape, BF16), pltpu.VMEM(weights.shape, BF16)]
        + [pltpu.SemaphoreType.DMA((2, chips_x)), pltpu.SemaphoreType.DMA],
        compiler_params=room(20),
        name="grads",
    )(lax.axis_index("core").reshape(1), lax.axis_index("yo").reshape(1), along_x, crossed, weights)
    met = lax.all_to_all(parts, GROUP, split_axis=0, concat_axis=0, tiled=True)
    grad_gate, grad_up, grad_down = pl.pallas_call(
        total_kernel,
        out_shape=[jax.ShapeDtypeStruct((units, features), BF16)] * 3,
        in_specs=[VMEM],
        out_specs=[VMEM] * 3,
        compiler_params=room(8),
        name="total",
    )(met)
    return grad_gate.T[None], grad_up.T[None], grad_down[None]


def solution(mesh, chips_x=CHIPS_X):
    section, ep = mesh.devices.shape
    shape = (section // (chips_x * CORES * PAIR), PAIR, chips_x, CORES, ep // PAIR, PAIR)
    fine = Mesh(mesh.devices.reshape(shape), SEC + EP)
    placed = (
        P(EP, SEC),
        P(EP, SEC),
        P(EP, None),
        P(EP, None),
        P(EP, None, SEC),
        P(EP, None, SEC),
        P(EP, SEC, None),
    )
    return jax.shard_map(
        shards,
        mesh=fine,
        in_specs=placed,
        out_specs=(P(EP, None, SEC), P(EP, None, SEC), P(EP, SEC, None)),
        check_vma=False,
    )
```

```python
import functools

import jax
import jax.numpy as jnp
from jax import lax
from jax.experimental import pallas as pl
from jax.experimental.pallas import tpu as pltpu
from jax.sharding import Mesh, PartitionSpec as P

BF16, F32 = jnp.bfloat16, jnp.float32
CORES = 2
CHIPS_X = 4
PAIR = 2
LANES = 128
SEC = ("zo", "zi", "x", "core")
EP = ("yo", "yi")
GROUP = ("zi", "yi")


def dot(a, b):
    return jnp.dot(a, b, preferred_element_type=F32)


def dot_t(a, b):
    return lax.dot_general(a, b, (((1,), (1,)), ((), ())), preferred_element_type=F32)


def spread(narrow_lane, wide_lane):
    return (narrow_lane == wide_lane - (wide_lane >> 4)) & ((wide_lane & 15) != 15)


def widen(rows, wide):
    narrow = rows.shape[1]
    pieces = []
    for start in range(0, wide, LANES):
        low = start - start // 16
        low = low // LANES * LANES
        high = min(narrow, low + 2 * LANES)
        source = lax.broadcasted_iota(jnp.int32, (high - low, LANES), 0) + low
        target = lax.broadcasted_iota(jnp.int32, (high - low, LANES), 1) + start
        chosen = spread(source, target).astype(F32).astype(BF16)
        pieces.append(dot(rows[:, low:high], chosen).astype(BF16))
    return jnp.concatenate(pieces, axis=1)


def narrowed(rows, narrow):
    wide = rows.shape[1]
    pieces = []
    for start in range(0, narrow, LANES):
        width = min(LANES, narrow - start)
        low = start // 15 * 16 // LANES * LANES
        last = start + width - 1
        high = min(wide, -(-(last // 15 * 16 + last % 15 + 1) // LANES) * LANES)
        source = lax.broadcasted_iota(jnp.int32, (high - low, width), 0) + low
        target = lax.broadcasted_iota(jnp.int32, (high - low, width), 1) + start
        chosen = spread(target, source).astype(F32).astype(BF16)
        pieces.append(dot(rows[:, low:high], chosen).astype(BF16))
    return jnp.concatenate(pieces, axis=1)


def half_turn(tile):
    return pltpu.roll(tile, LANES // 2, 1)


def turned(rows):
    tiles = [half_turn(rows[:, k : k + LANES]) for k in range(0, rows.shape[1], LANES)]
    return jnp.concatenate(tiles, axis=1)


def pack_kernel(zone, yi, tokens, cotangent, ids, probs, out):
    count = tokens.shape[1]
    mine = ids[...] == zone[0]
    weight = jnp.sum(jnp.where(mine, probs[...], 0.0), axis=0, keepdims=True)
    high = weight.astype(BF16).astype(F32)
    left = jnp.concatenate([tokens[...].astype(F32), high], axis=0)
    right = jnp.concatenate([cotangent[...].astype(F32), weight - high], axis=0)
    odd = yi[0] == 1
    first, second = jnp.where(odd, right, left), jnp.where(odd, left, right)
    lower = lax.broadcasted_iota(jnp.int32, (first.shape[0], LANES), 1) < LANES // 2
    for tile in range(count // LANES):
        a, b = first[:, tile * LANES : (tile + 1) * LANES], second[:, tile * LANES : (tile + 1) * LANES]
        quarters = (jnp.where(lower, a, half_turn(b)), jnp.where(lower, half_turn(a), b))
        for k, quarter in enumerate(quarters):
            zi, yi = divmod(2 * tile + k, PAIR)
            for yo in range(out.shape[1]):
                out[zi, yo, yi] = quarter.astype(BF16)


def weights_kernel(gate_w, up_w, down_w, out):
    hidden, wide = out.shape[0] // 3, out.shape[1]
    units = gate_w.shape[0]
    filler = jnp.zeros((hidden - units, gate_w.shape[1]), F32)
    rows = []
    for ref in (gate_w, up_w, down_w):
        rows += [ref[...].astype(F32), filler]
    out[...] = widen(jnp.concatenate(rows, axis=0).astype(BF16), wide)


def grads_kernel(core_at, x_at, yo_at, *refs):
    blocks, (weights, out, inputs, cotangents) = refs[:-4], refs[-4:]
    chips_x = len(blocks) // CORES
    chips_z, tokens_y, depth, lanes = blocks[0].shape
    groups, stacked, wide = weights.shape
    hidden = stacked // 3
    core, x, yo = core_at[0], x_at[0], yo_at[0]
    lower = lax.broadcasted_iota(jnp.int32, (chips_z, depth, lanes), 2) < lanes // 2
    for k, ref in enumerate(blocks):
        steps, crossed = divmod(k, CORES)
        slot = lax.rem(x + chips_x - steps, chips_x) * CORES + (1 - core if crossed else core)
        for pair in range(tokens_y // 2):
            even, odd = ref[:, 2 * pair], ref[:, 2 * pair + 1]
            at = slice(pair * lanes, (pair + 1) * lanes)
            inputs[:, slot, :, at] = jnp.where(lower, even, odd)
            cotangents[:, slot, :, at] = jnp.where(lower, odd, even)
    total = tokens_y // 2 * lanes
    rows = inputs[...].reshape(wide, total)
    backs = cotangents[...].reshape(wide, total)

    def part(k):
        return weights[:, k * hidden : (k + 1) * hidden, :].reshape(groups * hidden, wide)

    gate = dot(part(0), rows)
    linear = dot(part(1), rows)
    back = turned(dot(part(2), backs))
    shares = []
    for j in range(groups):
        expert = yo * PAIR + j % PAIR
        high = inputs[expert, 0].astype(F32)[depth - 1 : depth]
        low = turned(cotangents[expert, 0].astype(F32))[depth - 1 : depth]
        shares.append(jnp.broadcast_to(high + low, (hidden, total)))
    share = jnp.concatenate(shares, axis=0)
    back = back * share
    sigma = jax.nn.sigmoid(gate)
    lifted = turned(gate * sigma * linear * share).astype(BF16)
    gate_term = (back * linear * sigma * (1.0 + gate * (1.0 - sigma))).astype(BF16)
    linear_term = (back * gate * sigma).astype(BF16)
    for k, (left, right) in enumerate(((gate_term, rows), (linear_term, rows), (lifted, backs))):
        grad = dot_t(left, right).astype(BF16)
        out[:, k * hidden : (k + 1) * hidden, :] = grad.reshape(groups, hidden, wide)


def total_kernel(parts, gate_g, up_g, down_g):
    hidden = parts.shape[1] // 3
    total = parts[0].astype(F32)
    for j in range(1, parts.shape[0]):
        total = total + parts[j].astype(F32)
    units, narrow = gate_g.shape
    slim = narrowed(total.astype(BF16), narrow).astype(F32)
    for k, ref in enumerate((gate_g, up_g, down_g)):
        ref[...] = slim[k * hidden : k * hidden + units].astype(BF16)


VMEM = pl.BlockSpec(memory_space=pltpu.VMEM)
SMEM = pl.BlockSpec(memory_space=pltpu.SMEM)


def room(mib):
    return pltpu.CompilerParams(vmem_limit_bytes=mib * 1024 * 1024)


def swap(value, axis):
    return lax.ppermute(value, axis, [(0, 1), (1, 0)])


def shards(tokens, grad_out, expert_ids, probs, w_gate, w_up, w_down):
    pairs_z, chips_x, pairs_y = lax.axis_size("zo"), lax.axis_size("x"), lax.axis_size("yo")
    chips_z, groups = pairs_z * PAIR, PAIR * PAIR
    count, width = tokens.shape
    features, units = w_gate.shape[1:]
    depth = width + 1
    wide = chips_z * chips_x * CORES * depth
    hidden = -(-units // 16) * 16
    zone = lax.axis_index(("zo", "zi"))

    packed = pl.pallas_call(
        pack_kernel,
        out_shape=jax.ShapeDtypeStruct((PAIR, pairs_y, PAIR, depth, LANES), BF16),
        in_specs=[SMEM, SMEM, VMEM, VMEM, VMEM, VMEM],
        out_specs=VMEM,
        name="pack",
    )(zone.reshape(1), lax.axis_index("yi").reshape(1), tokens.T, grad_out.T, expert_ids.T, probs.T)
    stacked = pl.pallas_call(
        weights_kernel,
        out_shape=jax.ShapeDtypeStruct((3 * hidden, wide), BF16),
        in_specs=[VMEM] * 3,
        out_specs=VMEM,
        name="widen_weights",
    )(w_gate[0].T, w_up[0].T, w_down[0])
    sent = packed.reshape(PAIR * pairs_y * PAIR, depth, LANES)
    quarter = lax.all_to_all(sent, ("zi",) + EP, split_axis=0, concat_axis=0, tiled=True)
    quarter, stacked = lax.optimization_barrier((quarter, stacked))
    weights = lax.all_gather(stacked, GROUP)
    along_z = lax.all_gather(quarter, "zo").reshape(chips_z, pairs_y * PAIR, depth, LANES)
    blocks = []
    for steps in range(chips_x):
        along = [(i, (i + steps) % chips_x) for i in range(chips_x)]
        block = lax.ppermute(along_z, "x", along) if steps else along_z
        blocks += [block, swap(block, "core")]

    parts = pl.pallas_call(
        grads_kernel,
        out_shape=jax.ShapeDtypeStruct((groups, 3 * hidden, wide), BF16),
        in_specs=[SMEM] * 3 + [VMEM] * (len(blocks) + 1),
        out_specs=VMEM,
        scratch_shapes=[pltpu.VMEM((chips_z, chips_x * CORES, depth, pairs_y * LANES), BF16)] * 2,
        compiler_params=room(20),
        name="grads",
    )(*(lax.axis_index(axis).reshape(1) for axis in ("core", "x", "yo")), *blocks, weights)
    met = lax.all_to_all(parts, GROUP, split_axis=0, concat_axis=0, tiled=True)
    grad_gate, grad_up, grad_down = pl.pallas_call(
        total_kernel,
        out_shape=[jax.ShapeDtypeStruct((units, features), BF16)] * 3,
        in_specs=[VMEM],
        out_specs=[VMEM] * 3,
        compiler_params=room(8),
        name="total",
    )(met)
    return grad_gate.T[None], grad_up.T[None], grad_down[None]


def solution(mesh, chips_x=CHIPS_X):
    section, ep = mesh.devices.shape
    shape = (section // (chips_x * CORES * PAIR), PAIR, chips_x, CORES, ep // PAIR, PAIR)
    fine = Mesh(mesh.devices.reshape(shape), SEC + EP)
    placed = (
        P(EP, SEC),
        P(EP, SEC),
        P(EP, None),
        P(EP, None),
        P(EP, None, SEC),
        P(EP, None, SEC),
        P(EP, SEC, None),
    )
    return jax.shard_map(
        shards,
        mesh=fine,
        in_specs=placed,
        out_specs=(P(EP, None, SEC), P(EP, None, SEC), P(EP, SEC, None)),
        check_vma=False,
    )
```

```python
import functools

import jax
import jax.numpy as jnp
from jax import lax
from jax.experimental import pallas as pl
from jax.experimental.pallas import tpu as pltpu
from jax.sharding import Mesh, PartitionSpec as P

BF16, F32 = jnp.bfloat16, jnp.float32
CORES = 2
CHIPS_X = 4
PAIR = 2
LANES = 128
SEC = ("zo", "zi", "x", "core")
EP = ("yo", "yi")
GROUP = ("zi", "yi")


def dot(a, b):
    return jnp.dot(a, b, preferred_element_type=F32)


def dot_t(a, b):
    return lax.dot_general(a, b, (((1,), (1,)), ((), ())), preferred_element_type=F32)


def spread(narrow_lane, wide_lane):
    return (narrow_lane == wide_lane - (wide_lane >> 4)) & ((wide_lane & 15) != 15)


def widen(rows, wide):
    narrow = rows.shape[1]
    pieces = []
    for start in range(0, wide, LANES):
        low = start - start // 16
        low = low // LANES * LANES
        high = min(narrow, low + 2 * LANES)
        source = lax.broadcasted_iota(jnp.int32, (high - low, LANES), 0) + low
        target = lax.broadcasted_iota(jnp.int32, (high - low, LANES), 1) + start
        chosen = spread(source, target).astype(F32).astype(BF16)
        pieces.append(dot(rows[:, low:high], chosen).astype(BF16))
    return jnp.concatenate(pieces, axis=1)


def narrowed(rows, narrow):
    wide = rows.shape[1]
    pieces = []
    for start in range(0, narrow, LANES):
        width = min(LANES, narrow - start)
        low = start // 15 * 16 // LANES * LANES
        last = start + width - 1
        high = min(wide, -(-(last // 15 * 16 + last % 15 + 1) // LANES) * LANES)
        source = lax.broadcasted_iota(jnp.int32, (high - low, width), 0) + low
        target = lax.broadcasted_iota(jnp.int32, (high - low, width), 1) + start
        chosen = spread(target, source).astype(F32).astype(BF16)
        pieces.append(dot(rows[:, low:high], chosen).astype(BF16))
    return jnp.concatenate(pieces, axis=1)


def half_turn(tile):
    return pltpu.roll(tile, LANES // 2, 1)


def turned(rows):
    tiles = [half_turn(rows[:, k : k + LANES]) for k in range(0, rows.shape[1], LANES)]
    return jnp.concatenate(tiles, axis=1)


def pack_kernel(zone, yi, tokens, cotangent, ids, probs, out):
    count = tokens.shape[1]
    mine = ids[...] == zone[0]
    weight = jnp.sum(jnp.where(mine, probs[...], 0.0), axis=0, keepdims=True)
    high = weight.astype(BF16).astype(F32)
    left = jnp.concatenate([tokens[...].astype(F32), high], axis=0)
    right = jnp.concatenate([cotangent[...].astype(F32), weight - high], axis=0)
    odd = yi[0] == 1
    first, second = jnp.where(odd, right, left), jnp.where(odd, left, right)
    lower = lax.broadcasted_iota(jnp.int32, (first.shape[0], LANES), 1) < LANES // 2
    for tile in range(count // LANES):
        a, b = first[:, tile * LANES : (tile + 1) * LANES], second[:, tile * LANES : (tile + 1) * LANES]
        quarters = (jnp.where(lower, a, half_turn(b)), jnp.where(lower, half_turn(a), b))
        for k, quarter in enumerate(quarters):
            zi, yi = divmod(2 * tile + k, PAIR)
            for yo in range(out.shape[1]):
                out[zi, yo, yi] = quarter.astype(BF16)


def weights_kernel(gate_w, up_w, down_w, out):
    hidden, wide = out.shape[0] // 3, out.shape[1]
    units = gate_w.shape[0]
    filler = jnp.zeros((hidden - units, gate_w.shape[1]), F32)
    rows = []
    for ref in (gate_w, up_w, down_w):
        rows += [ref[...].astype(F32), filler]
    out[...] = widen(jnp.concatenate(rows, axis=0).astype(BF16), wide)


def grads_kernel(core_at, x_at, yo_at, zo_at, *refs):
    blocks, (weights, out, inputs, cotangents) = refs[:-4], refs[-4:]
    chips_x = len(blocks) // CORES
    chips_z, tokens_y, depth, lanes = blocks[0].shape
    groups, stacked, wide = weights.shape
    hidden = stacked // 3
    core, x, yo, zo = core_at[0], x_at[0], yo_at[0], zo_at[0]
    pairs_z = chips_z // PAIR
    lower = lax.broadcasted_iota(jnp.int32, (PAIR, depth, lanes), 2) < lanes // 2
    for k, ref in enumerate(blocks):
        steps, crossed = divmod(k, CORES)
        slot = lax.rem(x + chips_x - steps, chips_x) * CORES + (1 - core if crossed else core)
        for back in range(pairs_z):
            source = pl.ds(back * PAIR, PAIR)
            target = pl.ds(lax.rem(zo + pairs_z - back, pairs_z) * PAIR, PAIR)
            for pair in range(tokens_y // 2):
                even, odd = ref[source, 2 * pair], ref[source, 2 * pair + 1]
                at = slice(pair * lanes, (pair + 1) * lanes)
                inputs[target, slot, :, at] = jnp.where(lower, even, odd)
                cotangents[target, slot, :, at] = jnp.where(lower, odd, even)
    total = tokens_y // 2 * lanes
    rows = inputs[...].reshape(wide, total)
    backs = cotangents[...].reshape(wide, total)

    def part(k):
        return weights[:, k * hidden : (k + 1) * hidden, :].reshape(groups * hidden, wide)

    gate = dot(part(0), rows)
    linear = dot(part(1), rows)
    back = turned(dot(part(2), backs))
    shares = []
    for j in range(groups):
        expert = yo * PAIR + j % PAIR
        high = inputs[expert, 0].astype(F32)[depth - 1 : depth]
        low = turned(cotangents[expert, 0].astype(F32))[depth - 1 : depth]
        shares.append(jnp.broadcast_to(high + low, (hidden, total)))
    share = jnp.concatenate(shares, axis=0)
    back = back * share
    sigma = jax.nn.sigmoid(gate)
    lifted = turned(gate * sigma * linear * share).astype(BF16)
    gate_term = (back * linear * sigma * (1.0 + gate * (1.0 - sigma))).astype(BF16)
    linear_term = (back * gate * sigma).astype(BF16)
    for k, (left, right) in enumerate(((gate_term, rows), (linear_term, rows), (lifted, backs))):
        grad = dot_t(left, right).astype(BF16)
        out[:, k * hidden : (k + 1) * hidden, :] = grad.reshape(groups, hidden, wide)


def total_kernel(parts, gate_g, up_g, down_g):
    hidden = parts.shape[1] // 3
    total = parts[0].astype(F32)
    for j in range(1, parts.shape[0]):
        total = total + parts[j].astype(F32)
    units, narrow = gate_g.shape
    slim = narrowed(total.astype(BF16), narrow).astype(F32)
    for k, ref in enumerate((gate_g, up_g, down_g)):
        ref[...] = slim[k * hidden : k * hidden + units].astype(BF16)


VMEM = pl.BlockSpec(memory_space=pltpu.VMEM)
SMEM = pl.BlockSpec(memory_space=pltpu.SMEM)


def room(mib):
    return pltpu.CompilerParams(vmem_limit_bytes=mib * 1024 * 1024)


def swap(value, axis):
    return lax.ppermute(value, axis, [(0, 1), (1, 0)])


def ring(block, axis):
    size = lax.axis_size(axis)
    up = [(i, (i + 1) % size) for i in range(size)]
    down = [(j, i) for i, j in up]
    found = [block] + [None] * (size - 1)
    ahead = behind = block
    for step in range(1, size // 2 + 1):
        ahead = lax.ppermute(ahead, axis, up)
        found[step] = ahead
        if step < size - step:
            behind = lax.ppermute(behind, axis, down)
            found[size - step] = behind
    return found


def shards(tokens, grad_out, expert_ids, probs, w_gate, w_up, w_down):
    pairs_z, chips_x, pairs_y = lax.axis_size("zo"), lax.axis_size("x"), lax.axis_size("yo")
    chips_z, groups = pairs_z * PAIR, PAIR * PAIR
    count, width = tokens.shape
    features, units = w_gate.shape[1:]
    depth = width + 1
    wide = chips_z * chips_x * CORES * depth
    hidden = -(-units // 16) * 16
    zone = lax.axis_index(("zo", "zi"))

    packed = pl.pallas_call(
        pack_kernel,
        out_shape=jax.ShapeDtypeStruct((PAIR, pairs_y, PAIR, depth, LANES), BF16),
        in_specs=[SMEM, SMEM, VMEM, VMEM, VMEM, VMEM],
        out_specs=VMEM,
        name="pack",
    )(zone.reshape(1), lax.axis_index("yi").reshape(1), tokens.T, grad_out.T, expert_ids.T, probs.T)
    stacked = pl.pallas_call(
        weights_kernel,
        out_shape=jax.ShapeDtypeStruct((3 * hidden, wide), BF16),
        in_specs=[VMEM] * 3,
        out_specs=VMEM,
        name="widen_weights",
    )(w_gate[0].T, w_up[0].T, w_down[0])
    sent = packed.reshape(PAIR * pairs_y * PAIR, depth, LANES)
    quarter = lax.all_to_all(sent, ("zi",) + EP, split_axis=0, concat_axis=0, tiled=True)
    quarter, stacked = lax.optimization_barrier((quarter, stacked))
    weights = lax.all_gather(stacked, GROUP)
    along_z = jnp.stack(ring(quarter, "zo"))
    along_z = along_z.reshape(chips_z, pairs_y * PAIR, depth, LANES)
    blocks = []
    for steps in range(chips_x):
        along = [(i, (i + steps) % chips_x) for i in range(chips_x)]
        block = lax.ppermute(along_z, "x", along) if steps else along_z
        blocks += [block, swap(block, "core")]

    parts = pl.pallas_call(
        grads_kernel,
        out_shape=jax.ShapeDtypeStruct((groups, 3 * hidden, wide), BF16),
        in_specs=[SMEM] * 4 + [VMEM] * (len(blocks) + 1),
        out_specs=VMEM,
        scratch_shapes=[pltpu.VMEM((chips_z, chips_x * CORES, depth, pairs_y * LANES), BF16)] * 2,
        compiler_params=room(20),
        name="grads",
    )(*(lax.axis_index(axis).reshape(1) for axis in ("core", "x", "yo", "zo")), *blocks, weights)
    met = lax.all_to_all(parts, GROUP, split_axis=0, concat_axis=0, tiled=True)
    grad_gate, grad_up, grad_down = pl.pallas_call(
        total_kernel,
        out_shape=[jax.ShapeDtypeStruct((units, features), BF16)] * 3,
        in_specs=[VMEM],
        out_specs=[VMEM] * 3,
        compiler_params=room(8),
        name="total",
    )(met)
    return grad_gate.T[None], grad_up.T[None], grad_down[None]


def solution(mesh, chips_x=CHIPS_X):
    section, ep = mesh.devices.shape
    shape = (section // (chips_x * CORES * PAIR), PAIR, chips_x, CORES, ep // PAIR, PAIR)
    fine = Mesh(mesh.devices.reshape(shape), SEC + EP)
    placed = (
        P(EP, SEC),
        P(EP, SEC),
        P(EP, None),
        P(EP, None),
        P(EP, None, SEC),
        P(EP, None, SEC),
        P(EP, SEC, None),
    )
    return jax.shard_map(
        shards,
        mesh=fine,
        in_specs=placed,
        out_specs=(P(EP, None, SEC), P(EP, None, SEC), P(EP, SEC, None)),
        check_vma=False,
    )
```

```python
import functools

import jax
import jax.numpy as jnp
from jax import lax
from jax.experimental import pallas as pl
from jax.experimental.pallas import tpu as pltpu
from jax.sharding import Mesh, PartitionSpec as P

BF16, F32 = jnp.bfloat16, jnp.float32
CORES = 2
CHIPS_X = 4
PAIR = 2
LANES = 128
SEC = ("zo", "zi", "x", "core")
EP = ("yo", "yi")
GROUP = ("zi", "yi")


def dot(a, b):
    return jnp.dot(a, b, preferred_element_type=F32)


def dot_t(a, b):
    return lax.dot_general(a, b, (((1,), (1,)), ((), ())), preferred_element_type=F32)


def spread(narrow_lane, wide_lane):
    return (narrow_lane == wide_lane - (wide_lane >> 4)) & ((wide_lane & 15) != 15)


def widen(rows, wide):
    narrow = rows.shape[1]
    pieces = []
    for start in range(0, wide, LANES):
        low = start - start // 16
        low = low // LANES * LANES
        high = min(narrow, low + 2 * LANES)
        source = lax.broadcasted_iota(jnp.int32, (high - low, LANES), 0) + low
        target = lax.broadcasted_iota(jnp.int32, (high - low, LANES), 1) + start
        chosen = spread(source, target).astype(F32).astype(BF16)
        pieces.append(dot(rows[:, low:high], chosen).astype(BF16))
    return jnp.concatenate(pieces, axis=1)


def narrowed(rows, narrow):
    wide = rows.shape[1]
    pieces = []
    for start in range(0, narrow, LANES):
        width = min(LANES, narrow - start)
        low = start // 15 * 16 // LANES * LANES
        last = start + width - 1
        high = min(wide, -(-(last // 15 * 16 + last % 15 + 1) // LANES) * LANES)
        source = lax.broadcasted_iota(jnp.int32, (high - low, width), 0) + low
        target = lax.broadcasted_iota(jnp.int32, (high - low, width), 1) + start
        chosen = spread(target, source).astype(F32).astype(BF16)
        pieces.append(dot(rows[:, low:high], chosen).astype(BF16))
    return jnp.concatenate(pieces, axis=1)


def half_turn(tile):
    return pltpu.roll(tile, LANES // 2, 1)


def turned(rows):
    tiles = [half_turn(rows[:, k : k + LANES]) for k in range(0, rows.shape[1], LANES)]
    return jnp.concatenate(tiles, axis=1)


def pack_kernel(zone, yi, tokens, cotangent, ids, probs, out):
    count = tokens.shape[1]
    mine = ids[...] == zone[0]
    weight = jnp.sum(jnp.where(mine, probs[...], 0.0), axis=0, keepdims=True)
    high = weight.astype(BF16).astype(F32)
    left = jnp.concatenate([tokens[...].astype(F32), high], axis=0)
    right = jnp.concatenate([cotangent[...].astype(F32), weight - high], axis=0)
    odd = yi[0] == 1
    first, second = jnp.where(odd, right, left), jnp.where(odd, left, right)
    lower = lax.broadcasted_iota(jnp.int32, (first.shape[0], LANES), 1) < LANES // 2
    for tile in range(count // LANES):
        a, b = first[:, tile * LANES : (tile + 1) * LANES], second[:, tile * LANES : (tile + 1) * LANES]
        quarters = (jnp.where(lower, a, half_turn(b)), jnp.where(lower, half_turn(a), b))
        for k, quarter in enumerate(quarters):
            zi, yi = divmod(2 * tile + k, PAIR)
            for yo in range(out.shape[1]):
                out[zi, yo, yi] = quarter.astype(BF16)


def weights_kernel(gate_w, up_w, down_w, out):
    hidden, wide = out.shape[0] // 3, out.shape[1]
    units = gate_w.shape[0]
    filler = jnp.zeros((hidden - units, gate_w.shape[1]), F32)
    rows = []
    for ref in (gate_w, up_w, down_w):
        rows += [ref[...].astype(F32), filler]
    out[...] = widen(jnp.concatenate(rows, axis=0).astype(BF16), wide)


def regroup_kernel(gathered, out):
    groups, stacked, wide = gathered.shape
    hidden = stacked // 3
    for k in range(3):
        out[k] = gathered[:, k * hidden : (k + 1) * hidden].reshape(groups * hidden, wide)


def grads_kernel(core_at, x_at, yo_at, *refs):
    blocks, (weights, out, inputs, cotangents) = refs[:-4], refs[-4:]
    chips_x = len(blocks) // CORES
    chips_z, tokens_y, depth, lanes = blocks[0].shape
    wide = weights.shape[2]
    groups, hidden = out.shape[0], out.shape[1] // 3
    core, x, yo = core_at[0], x_at[0], yo_at[0]
    lower = lax.broadcasted_iota(jnp.int32, (chips_z, depth, lanes), 2) < lanes // 2
    for k, ref in enumerate(blocks):
        steps, crossed = divmod(k, CORES)
        slot = lax.rem(x + chips_x - steps, chips_x) * CORES + (1 - core if crossed else core)
        for pair in range(tokens_y // 2):
            even, odd = ref[:, 2 * pair], ref[:, 2 * pair + 1]
            at = slice(pair * lanes, (pair + 1) * lanes)
            inputs[:, slot, :, at] = jnp.where(lower, even, odd)
            cotangents[:, slot, :, at] = jnp.where(lower, odd, even)
    total = tokens_y // 2 * lanes
    rows = inputs[...].reshape(wide, total)
    backs = cotangents[...].reshape(wide, total)

    units = groups * hidden
    both = dot(weights[:2].reshape(2 * units, wide), rows)
    gate, linear = both[:units], both[units:]
    back = turned(dot(weights[2], backs))
    shares = []
    for j in range(groups):
        expert = yo * PAIR + j % PAIR
        high = inputs[expert, 0].astype(F32)[depth - 1 : depth]
        low = turned(cotangents[expert, 0].astype(F32))[depth - 1 : depth]
        shares.append(jnp.broadcast_to(high + low, (hidden, total)))
    share = jnp.concatenate(shares, axis=0)
    back = back * share
    sigma = jax.nn.sigmoid(gate)
    lifted = turned(gate * sigma * linear * share).astype(BF16)
    gate_term = (back * linear * sigma * (1.0 + gate * (1.0 - sigma))).astype(BF16)
    linear_term = (back * gate * sigma).astype(BF16)
    upward = dot_t(jnp.concatenate([gate_term, linear_term], axis=0), rows).astype(BF16)
    grads = (upward[:units], upward[units:], dot_t(lifted, backs).astype(BF16))
    for k, grad in enumerate(grads):
        out[:, k * hidden : (k + 1) * hidden, :] = grad.reshape(groups, hidden, wide)


def total_kernel(parts, gate_g, up_g, down_g):
    hidden = parts.shape[1] // 3
    total = parts[0].astype(F32)
    for j in range(1, parts.shape[0]):
        total = total + parts[j].astype(F32)
    units, narrow = gate_g.shape
    slim = narrowed(total.astype(BF16), narrow).astype(F32)
    for k, ref in enumerate((gate_g, up_g, down_g)):
        ref[...] = slim[k * hidden : k * hidden + units].astype(BF16)


VMEM = pl.BlockSpec(memory_space=pltpu.VMEM)
SMEM = pl.BlockSpec(memory_space=pltpu.SMEM)


def room(mib):
    return pltpu.CompilerParams(vmem_limit_bytes=mib * 1024 * 1024)


def swap(value, axis):
    return lax.ppermute(value, axis, [(0, 1), (1, 0)])


def shards(tokens, grad_out, expert_ids, probs, w_gate, w_up, w_down):
    pairs_z, chips_x, pairs_y = lax.axis_size("zo"), lax.axis_size("x"), lax.axis_size("yo")
    chips_z, groups = pairs_z * PAIR, PAIR * PAIR
    count, width = tokens.shape
    features, units = w_gate.shape[1:]
    depth = width + 1
    wide = chips_z * chips_x * CORES * depth
    hidden = -(-units // 16) * 16
    zone = lax.axis_index(("zo", "zi"))

    packed = pl.pallas_call(
        pack_kernel,
        out_shape=jax.ShapeDtypeStruct((PAIR, pairs_y, PAIR, depth, LANES), BF16),
        in_specs=[SMEM, SMEM, VMEM, VMEM, VMEM, VMEM],
        out_specs=VMEM,
        name="pack",
    )(zone.reshape(1), lax.axis_index("yi").reshape(1), tokens.T, grad_out.T, expert_ids.T, probs.T)
    stacked = pl.pallas_call(
        weights_kernel,
        out_shape=jax.ShapeDtypeStruct((3 * hidden, wide), BF16),
        in_specs=[VMEM] * 3,
        out_specs=VMEM,
        name="widen_weights",
    )(w_gate[0].T, w_up[0].T, w_down[0])
    sent = packed.reshape(PAIR * pairs_y * PAIR, depth, LANES)
    quarter = lax.all_to_all(sent, ("zi",) + EP, split_axis=0, concat_axis=0, tiled=True)
    quarter, stacked = lax.optimization_barrier((quarter, stacked))
    weights = lax.all_gather(stacked, GROUP)
    along_z = lax.all_gather(quarter, "zo").reshape(chips_z, pairs_y * PAIR, depth, LANES)
    blocks = []
    for steps in range(chips_x):
        along = [(i, (i + steps) % chips_x) for i in range(chips_x)]
        block = lax.ppermute(along_z, "x", along) if steps else along_z
        blocks += [block, swap(block, "core")]

    regrouped = pl.pallas_call(
        regroup_kernel,
        out_shape=jax.ShapeDtypeStruct((3, groups * hidden, wide), BF16),
        in_specs=[VMEM],
        out_specs=VMEM,
        compiler_params=room(4),
        cost_estimate=pl.CostEstimate(flops=0, bytes_accessed=2 * 3 * groups * hidden * wide * 2, transcendentals=0),
        name="regroup",
    )(weights)
    parts = pl.pallas_call(
        grads_kernel,
        out_shape=jax.ShapeDtypeStruct((groups, 3 * hidden, wide), BF16),
        in_specs=[SMEM] * 3 + [VMEM] * (len(blocks) + 1),
        out_specs=VMEM,
        scratch_shapes=[pltpu.VMEM((chips_z, chips_x * CORES, depth, pairs_y * LANES), BF16)] * 2,
        compiler_params=room(20),
        name="grads",
    )(*(lax.axis_index(axis).reshape(1) for axis in ("core", "x", "yo")), *blocks, regrouped)
    met = lax.all_to_all(parts, GROUP, split_axis=0, concat_axis=0, tiled=True)
    grad_gate, grad_up, grad_down = pl.pallas_call(
        total_kernel,
        out_shape=[jax.ShapeDtypeStruct((units, features), BF16)] * 3,
        in_specs=[VMEM],
        out_specs=[VMEM] * 3,
        compiler_params=room(8),
        name="total",
    )(met)
    return grad_gate.T[None], grad_up.T[None], grad_down[None]


def solution(mesh, chips_x=CHIPS_X):
    section, ep = mesh.devices.shape
    shape = (section // (chips_x * CORES * PAIR), PAIR, chips_x, CORES, ep // PAIR, PAIR)
    fine = Mesh(mesh.devices.reshape(shape), SEC + EP)
    placed = (
        P(EP, SEC),
        P(EP, SEC),
        P(EP, None),
        P(EP, None),
        P(EP, None, SEC),
        P(EP, None, SEC),
        P(EP, SEC, None),
    )
    return jax.shard_map(
        shards,
        mesh=fine,
        in_specs=placed,
        out_specs=(P(EP, None, SEC), P(EP, None, SEC), P(EP, SEC, None)),
        check_vma=False,
    )
```

```python
import functools

import jax
import jax.numpy as jnp
from jax import lax
from jax.experimental import pallas as pl
from jax.experimental.pallas import tpu as pltpu
from jax.sharding import Mesh, PartitionSpec as P

BF16, F32 = jnp.bfloat16, jnp.float32
CORES = 2
CHIPS_X = 4
PAIR = 2
LANES = 128
SEC = ("zo", "zi", "x", "core")
EP = ("yo", "yi")
GROUP = ("zi", "yi")


def dot(a, b):
    return jnp.dot(a, b, preferred_element_type=F32)


def dot_t(a, b):
    return lax.dot_general(a, b, (((1,), (1,)), ((), ())), preferred_element_type=F32)


def spread(narrow_lane, wide_lane):
    return (narrow_lane == wide_lane - (wide_lane >> 4)) & ((wide_lane & 15) != 15)


def widen(rows, wide):
    narrow = rows.shape[1]
    pieces = []
    for start in range(0, wide, LANES):
        low = start - start // 16
        low = low // LANES * LANES
        high = min(narrow, low + 2 * LANES)
        source = lax.broadcasted_iota(jnp.int32, (high - low, LANES), 0) + low
        target = lax.broadcasted_iota(jnp.int32, (high - low, LANES), 1) + start
        chosen = spread(source, target).astype(F32).astype(BF16)
        pieces.append(dot(rows[:, low:high], chosen).astype(BF16))
    return jnp.concatenate(pieces, axis=1)


def narrowed(rows, narrow):
    wide = rows.shape[1]
    pieces = []
    for start in range(0, narrow, LANES):
        width = min(LANES, narrow - start)
        low = start // 15 * 16 // LANES * LANES
        last = start + width - 1
        high = min(wide, -(-(last // 15 * 16 + last % 15 + 1) // LANES) * LANES)
        source = lax.broadcasted_iota(jnp.int32, (high - low, width), 0) + low
        target = lax.broadcasted_iota(jnp.int32, (high - low, width), 1) + start
        chosen = spread(target, source).astype(F32).astype(BF16)
        pieces.append(dot(rows[:, low:high], chosen).astype(BF16))
    return jnp.concatenate(pieces, axis=1)


def half_turn(tile):
    return pltpu.roll(tile, LANES // 2, 1)


def turned(rows):
    tiles = [half_turn(rows[:, k : k + LANES]) for k in range(0, rows.shape[1], LANES)]
    return jnp.concatenate(tiles, axis=1)


def dense(grads, narrow, tall):
    wide, whole = grads[0].shape[1], narrow // LANES * LANES
    rest = narrow - whole
    columns = [[] for _ in grads]
    shared = 0.0
    for k, grad in enumerate(grads):
        main = narrowed(grad, whole)
        columns[k] = [main[:, at : at + LANES] for at in range(0, whole, LANES)]
        low = (whole // 15 * 16) // LANES * LANES
        source = lax.broadcasted_iota(jnp.int32, (wide - low, LANES), 0) + low
        target = lax.broadcasted_iota(jnp.int32, (wide - low, LANES), 1) - k * rest
        chosen = spread(target + whole, source) & (target >= 0) & (target < rest)
        shared = shared + dot(grad[:, low:], chosen.astype(F32).astype(BF16))
    return columns, shared.astype(BF16)


def pack_kernel(zone, yi, tokens, cotangent, ids, probs, out):
    count = tokens.shape[1]
    mine = ids[...] == zone[0]
    weight = jnp.sum(jnp.where(mine, probs[...], 0.0), axis=0, keepdims=True)
    high = weight.astype(BF16).astype(F32)
    left = jnp.concatenate([tokens[...].astype(F32), high], axis=0)
    right = jnp.concatenate([cotangent[...].astype(F32), weight - high], axis=0)
    odd = yi[0] == 1
    first, second = jnp.where(odd, right, left), jnp.where(odd, left, right)
    lower = lax.broadcasted_iota(jnp.int32, (first.shape[0], LANES), 1) < LANES // 2
    for tile in range(count // LANES):
        a, b = first[:, tile * LANES : (tile + 1) * LANES], second[:, tile * LANES : (tile + 1) * LANES]
        quarters = (jnp.where(lower, a, half_turn(b)), jnp.where(lower, half_turn(a), b))
        for k, quarter in enumerate(quarters):
            zi, yi = divmod(2 * tile + k, PAIR)
            for yo in range(out.shape[1]):
                out[zi, yo, yi] = quarter.astype(BF16)


def weights_kernel(gate_w, up_w, down_w, out):
    hidden, wide = out.shape[0] // 3, out.shape[1]
    units = gate_w.shape[0]
    filler = jnp.zeros((hidden - units, gate_w.shape[1]), F32)
    rows = []
    for ref in (gate_w, up_w, down_w):
        rows += [ref[...].astype(F32), filler]
    out[...] = widen(jnp.concatenate(rows, axis=0).astype(BF16), wide)


def regroup_kernel(gathered, out):
    groups, stacked, wide = gathered.shape
    hidden = stacked // 3
    for k in range(3):
        out[k] = gathered[:, k * hidden : (k + 1) * hidden].reshape(groups * hidden, wide)


def grads_kernel(narrow, hidden, core_at, x_at, yo_at, *refs):
    blocks, (weights, out, inputs, cotangents) = refs[:-4], refs[-4:]
    chips_x = len(blocks) // CORES
    chips_z, tokens_y, depth, lanes = blocks[0].shape
    wide = weights.shape[2]
    groups = out.shape[0]
    core, x, yo = core_at[0], x_at[0], yo_at[0]
    lower = lax.broadcasted_iota(jnp.int32, (chips_z, depth, lanes), 2) < lanes // 2
    for k, ref in enumerate(blocks):
        steps, crossed = divmod(k, CORES)
        slot = lax.rem(x + chips_x - steps, chips_x) * CORES + (1 - core if crossed else core)
        for pair in range(tokens_y // 2):
            even, odd = ref[:, 2 * pair], ref[:, 2 * pair + 1]
            at = slice(pair * lanes, (pair + 1) * lanes)
            inputs[:, slot, :, at] = jnp.where(lower, even, odd)
            cotangents[:, slot, :, at] = jnp.where(lower, odd, even)
    total = tokens_y // 2 * lanes
    rows = inputs[...].reshape(wide, total)
    backs = cotangents[...].reshape(wide, total)

    units = groups * hidden
    both = dot(weights[:2].reshape(2 * units, wide), rows)
    gate, linear = both[:units], both[units:]
    back = turned(dot(weights[2], backs))
    shares = []
    for j in range(groups):
        expert = yo * PAIR + j % PAIR
        high = inputs[expert, 0].astype(F32)[depth - 1 : depth]
        low = turned(cotangents[expert, 0].astype(F32))[depth - 1 : depth]
        shares.append(jnp.broadcast_to(high + low, (hidden, total)))
    share = jnp.concatenate(shares, axis=0)
    back = back * share
    sigma = jax.nn.sigmoid(gate)
    lifted = turned(gate * sigma * linear * share).astype(BF16)
    gate_term = (back * linear * sigma * (1.0 + gate * (1.0 - sigma))).astype(BF16)
    linear_term = (back * gate * sigma).astype(BF16)
    upward = dot_t(jnp.concatenate([gate_term, linear_term], axis=0), rows).astype(BF16)
    grads = (upward[:units], upward[units:], dot_t(lifted, backs).astype(BF16))
    tall = 16
    columns, shared = dense(grads, narrow, tall)
    halves = hidden // tall
    for j in range(groups):
        block = 0
        for column in sum(columns, []) + [shared]:
            for half in range(halves):
                at = j * hidden + half * tall
                out[j, block] = column[at : at + tall]
                block += 1


def total_kernel(parts, *refs):
    total = parts[0].astype(F32)
    for j in range(1, parts.shape[0]):
        total = total + parts[j].astype(F32)
    units, narrow = refs[0].shape
    whole = narrow // LANES
    rest, tall = narrow - whole * LANES, total.shape[1]
    halves = -(-units // tall)
    for half in range(halves):
        at = slice(half * tall, min(units, (half + 1) * tall))
        height = at.stop - at.start
        shared = total[len(refs) * whole * halves + half]
        for k, ref in enumerate(refs):
            for tile in range(whole):
                piece = total[(k * whole + tile) * halves + half]
                ref[at, tile * LANES : (tile + 1) * LANES] = piece[:height].astype(BF16)
            turn = pltpu.roll(shared, LANES - k * rest, 1) if k else shared
            ref[at, whole * LANES :] = turn[:height, :rest].astype(BF16)


VMEM = pl.BlockSpec(memory_space=pltpu.VMEM)
SMEM = pl.BlockSpec(memory_space=pltpu.SMEM)


def room(mib):
    return pltpu.CompilerParams(vmem_limit_bytes=mib * 1024 * 1024)


def swap(value, axis):
    return lax.ppermute(value, axis, [(0, 1), (1, 0)])


def shards(tokens, grad_out, expert_ids, probs, w_gate, w_up, w_down):
    pairs_z, chips_x, pairs_y = lax.axis_size("zo"), lax.axis_size("x"), lax.axis_size("yo")
    chips_z, groups = pairs_z * PAIR, PAIR * PAIR
    count, width = tokens.shape
    features, units = w_gate.shape[1:]
    depth = width + 1
    wide = chips_z * chips_x * CORES * depth
    hidden = -(-units // 16) * 16
    zone = lax.axis_index(("zo", "zi"))

    packed = pl.pallas_call(
        pack_kernel,
        out_shape=jax.ShapeDtypeStruct((PAIR, pairs_y, PAIR, depth, LANES), BF16),
        in_specs=[SMEM, SMEM, VMEM, VMEM, VMEM, VMEM],
        out_specs=VMEM,
        name="pack",
    )(zone.reshape(1), lax.axis_index("yi").reshape(1), tokens.T, grad_out.T, expert_ids.T, probs.T)
    stacked = pl.pallas_call(
        weights_kernel,
        out_shape=jax.ShapeDtypeStruct((3 * hidden, wide), BF16),
        in_specs=[VMEM] * 3,
        out_specs=VMEM,
        name="widen_weights",
    )(w_gate[0].T, w_up[0].T, w_down[0])
    sent = packed.reshape(PAIR * pairs_y * PAIR, depth, LANES)
    quarter = lax.all_to_all(sent, ("zi",) + EP, split_axis=0, concat_axis=0, tiled=True)
    quarter, stacked = lax.optimization_barrier((quarter, stacked))
    weights = lax.all_gather(stacked, GROUP)
    along_z = lax.all_gather(quarter, "zo").reshape(chips_z, pairs_y * PAIR, depth, LANES)
    blocks = []
    for steps in range(chips_x):
        along = [(i, (i + steps) % chips_x) for i in range(chips_x)]
        block = lax.ppermute(along_z, "x", along) if steps else along_z
        blocks += [block, swap(block, "core")]

    regrouped = pl.pallas_call(
        regroup_kernel,
        out_shape=jax.ShapeDtypeStruct((3, groups * hidden, wide), BF16),
        in_specs=[VMEM],
        out_specs=VMEM,
        compiler_params=room(4),
        cost_estimate=pl.CostEstimate(flops=0, bytes_accessed=2 * 3 * groups * hidden * wide * 2, transcendentals=0),
        name="regroup",
    )(weights)
    sent_blocks = (3 * (features // LANES) + 1) * hidden // 16
    parts = pl.pallas_call(
        functools.partial(grads_kernel, features, hidden),
        out_shape=jax.ShapeDtypeStruct((groups, sent_blocks, 16, LANES), BF16),
        in_specs=[SMEM] * 3 + [VMEM] * (len(blocks) + 1),
        out_specs=VMEM,
        scratch_shapes=[pltpu.VMEM((chips_z, chips_x * CORES, depth, pairs_y * LANES), BF16)] * 2,
        compiler_params=room(20),
        name="grads",
    )(*(lax.axis_index(axis).reshape(1) for axis in ("core", "x", "yo")), *blocks, regrouped)
    met = lax.all_to_all(parts, GROUP, split_axis=0, concat_axis=0, tiled=True)
    grad_gate, grad_up, grad_down = pl.pallas_call(
        total_kernel,
        out_shape=[jax.ShapeDtypeStruct((units, features), BF16)] * 3,
        in_specs=[VMEM],
        out_specs=[VMEM] * 3,
        compiler_params=room(8),
        name="total",
    )(met)
    return grad_gate.T[None], grad_up.T[None], grad_down[None]


def solution(mesh, chips_x=CHIPS_X):
    section, ep = mesh.devices.shape
    shape = (section // (chips_x * CORES * PAIR), PAIR, chips_x, CORES, ep // PAIR, PAIR)
    fine = Mesh(mesh.devices.reshape(shape), SEC + EP)
    placed = (
        P(EP, SEC),
        P(EP, SEC),
        P(EP, None),
        P(EP, None),
        P(EP, None, SEC),
        P(EP, None, SEC),
        P(EP, SEC, None),
    )
    return jax.shard_map(
        shards,
        mesh=fine,
        in_specs=placed,
        out_specs=(P(EP, None, SEC), P(EP, None, SEC), P(EP, SEC, None)),
        check_vma=False,
    )
```

```python
import functools

import jax
import jax.numpy as jnp
from jax import lax
from jax.experimental import pallas as pl
from jax.experimental.pallas import tpu as pltpu
from jax.sharding import Mesh, PartitionSpec as P

BF16, F32 = jnp.bfloat16, jnp.float32
CORES = 2
CHIPS_X = 4
PAIR = 2
LANES = 128
SEC = ("zo", "zi", "x", "core")
EP = ("yo", "yi")
GROUP = ("zi", "yi")


def dot(a, b):
    return jnp.dot(a, b, preferred_element_type=F32)


def dot_t(a, b):
    return lax.dot_general(a, b, (((1,), (1,)), ((), ())), preferred_element_type=F32)


def spread(narrow_lane, wide_lane):
    return (narrow_lane == wide_lane - (wide_lane >> 4)) & ((wide_lane & 15) != 15)


def widen(rows, wide):
    narrow = rows.shape[1]
    pieces = []
    for start in range(0, wide, LANES):
        low = start - start // 16
        low = low // LANES * LANES
        high = min(narrow, low + 2 * LANES)
        source = lax.broadcasted_iota(jnp.int32, (high - low, LANES), 0) + low
        target = lax.broadcasted_iota(jnp.int32, (high - low, LANES), 1) + start
        chosen = spread(source, target).astype(F32).astype(BF16)
        pieces.append(dot(rows[:, low:high], chosen).astype(BF16))
    return jnp.concatenate(pieces, axis=1)


def narrowed(rows, narrow):
    wide = rows.shape[1]
    pieces = []
    for start in range(0, narrow, LANES):
        width = min(LANES, narrow - start)
        low = start // 15 * 16 // LANES * LANES
        last = start + width - 1
        high = min(wide, -(-(last // 15 * 16 + last % 15 + 1) // LANES) * LANES)
        source = lax.broadcasted_iota(jnp.int32, (high - low, width), 0) + low
        target = lax.broadcasted_iota(jnp.int32, (high - low, width), 1) + start
        chosen = spread(target, source).astype(F32).astype(BF16)
        pieces.append(dot(rows[:, low:high], chosen).astype(BF16))
    return jnp.concatenate(pieces, axis=1)


def half_turn(tile):
    return pltpu.roll(tile, LANES // 2, 1)


def turned(rows):
    tiles = [half_turn(rows[:, k : k + LANES]) for k in range(0, rows.shape[1], LANES)]
    return jnp.concatenate(tiles, axis=1)


def dense(grads, narrow):
    wide, whole = grads[0].shape[1], narrow // LANES * LANES
    rest = narrow - whole
    main = narrowed(jnp.concatenate(grads, axis=0), whole)
    count = grads[0].shape[0]
    columns = []
    shared = 0.0
    for k, grad in enumerate(grads):
        columns.append([main[k * count : (k + 1) * count, at : at + LANES] for at in range(0, whole, LANES)])
        low = (whole // 15 * 16) // LANES * LANES
        source = lax.broadcasted_iota(jnp.int32, (wide - low, LANES), 0) + low
        target = lax.broadcasted_iota(jnp.int32, (wide - low, LANES), 1) - k * rest
        chosen = spread(target + whole, source) & (target >= 0) & (target < rest)
        shared = shared + dot(grad[:, low:], chosen.astype(F32).astype(BF16))
    return columns, shared.astype(BF16)


def pack_kernel(zone, yi, tokens, cotangent, ids, probs, out):
    count = tokens.shape[1]
    mine = ids[...] == zone[0]
    weight = jnp.sum(jnp.where(mine, probs[...], 0.0), axis=0, keepdims=True)
    high = weight.astype(BF16).astype(F32)
    left = jnp.concatenate([tokens[...].astype(F32), high], axis=0)
    right = jnp.concatenate([cotangent[...].astype(F32), weight - high], axis=0)
    odd = yi[0] == 1
    first, second = jnp.where(odd, right, left), jnp.where(odd, left, right)
    lower = lax.broadcasted_iota(jnp.int32, (first.shape[0], LANES), 1) < LANES // 2
    for tile in range(count // LANES):
        a, b = first[:, tile * LANES : (tile + 1) * LANES], second[:, tile * LANES : (tile + 1) * LANES]
        quarters = (jnp.where(lower, a, half_turn(b)), jnp.where(lower, half_turn(a), b))
        for k, quarter in enumerate(quarters):
            zi, yi = divmod(2 * tile + k, PAIR)
            for yo in range(out.shape[1]):
                out[zi, yo, yi] = quarter.astype(BF16)


def weights_kernel(gate_w, up_w, down_w, out):
    hidden, wide = out.shape[0] // 3, out.shape[1]
    units = gate_w.shape[0]
    filler = jnp.zeros((hidden - units, gate_w.shape[1]), F32)
    rows = []
    for ref in (gate_w, up_w, down_w):
        rows += [ref[...].astype(F32), filler]
    out[...] = widen(jnp.concatenate(rows, axis=0).astype(BF16), wide)


def regroup_kernel(gathered, out):
    groups, stacked, wide = gathered.shape
    hidden = stacked // 3
    for k in range(3):
        out[k] = gathered[:, k * hidden : (k + 1) * hidden].reshape(groups * hidden, wide)


def grads_kernel(narrow, hidden, core_at, x_at, yo_at, *refs):
    blocks, (weights, out, inputs, cotangents) = refs[:-4], refs[-4:]
    chips_x = len(blocks) // CORES
    chips_z, tokens_y, depth, lanes = blocks[0].shape
    wide = weights.shape[2]
    groups = out.shape[0]
    core, x, yo = core_at[0], x_at[0], yo_at[0]
    lower = lax.broadcasted_iota(jnp.int32, (chips_z, depth, lanes), 2) < lanes // 2
    for k, ref in enumerate(blocks):
        steps, crossed = divmod(k, CORES)
        slot = lax.rem(x + chips_x - steps, chips_x) * CORES + (1 - core if crossed else core)
        for pair in range(tokens_y // 2):
            even, odd = ref[:, 2 * pair], ref[:, 2 * pair + 1]
            at = slice(pair * lanes, (pair + 1) * lanes)
            inputs[:, slot, :, at] = jnp.where(lower, even, odd)
            cotangents[:, slot, :, at] = jnp.where(lower, odd, even)
    total = tokens_y // 2 * lanes
    rows = inputs[...].reshape(wide, total)
    backs = cotangents[...].reshape(wide, total)

    units = groups * hidden
    both = dot(weights[:2].reshape(2 * units, wide), rows)
    gate, linear = both[:units], both[units:]
    back = turned(dot(weights[2], backs))
    shares = []
    for j in range(groups):
        expert = yo * PAIR + j % PAIR
        high = inputs[expert, 0].astype(F32)[depth - 1 : depth]
        low = turned(cotangents[expert, 0].astype(F32))[depth - 1 : depth]
        shares.append(jnp.broadcast_to(high + low, (hidden, total)))
    share = jnp.concatenate(shares, axis=0)
    back = back * share
    sigma = jax.nn.sigmoid(gate)
    lifted = turned(gate * sigma * linear * share).astype(BF16)
    gate_term = (back * linear * sigma * (1.0 + gate * (1.0 - sigma))).astype(BF16)
    linear_term = (back * gate * sigma).astype(BF16)
    upward = dot_t(jnp.concatenate([gate_term, linear_term], axis=0), rows).astype(BF16)
    grads = (upward[:units], upward[units:], dot_t(lifted, backs).astype(BF16))
    tall = 16
    columns, shared = dense(grads, narrow)
    halves = hidden // tall
    for j in range(groups):
        block = 0
        for column in sum(columns, []) + [shared]:
            for half in range(halves):
                at = j * hidden + half * tall
                out[j, block] = column[at : at + tall]
                block += 1


def total_kernel(parts, *refs):
    total = parts[0].astype(F32)
    for j in range(1, parts.shape[0]):
        total = total + parts[j].astype(F32)
    units, narrow = refs[0].shape
    whole = narrow // LANES
    rest, tall = narrow - whole * LANES, total.shape[1]
    halves = -(-units // tall)
    for half in range(halves):
        at = slice(half * tall, min(units, (half + 1) * tall))
        height = at.stop - at.start
        shared = total[len(refs) * whole * halves + half]
        for k, ref in enumerate(refs):
            for tile in range(whole):
                piece = total[(k * whole + tile) * halves + half]
                ref[at, tile * LANES : (tile + 1) * LANES] = piece[:height].astype(BF16)
            turn = pltpu.roll(shared, LANES - k * rest, 1) if k else shared
            ref[at, whole * LANES :] = turn[:height, :rest].astype(BF16)


VMEM = pl.BlockSpec(memory_space=pltpu.VMEM)
SMEM = pl.BlockSpec(memory_space=pltpu.SMEM)


def room(mib):
    return pltpu.CompilerParams(vmem_limit_bytes=mib * 1024 * 1024)


def swap(value, axis):
    return lax.ppermute(value, axis, [(0, 1), (1, 0)])


def shards(tokens, grad_out, expert_ids, probs, w_gate, w_up, w_down):
    pairs_z, chips_x, pairs_y = lax.axis_size("zo"), lax.axis_size("x"), lax.axis_size("yo")
    chips_z, groups = pairs_z * PAIR, PAIR * PAIR
    count, width = tokens.shape
    features, units = w_gate.shape[1:]
    depth = width + 1
    wide = chips_z * chips_x * CORES * depth
    hidden = -(-units // 16) * 16
    zone = lax.axis_index(("zo", "zi"))

    packed = pl.pallas_call(
        pack_kernel,
        out_shape=jax.ShapeDtypeStruct((PAIR, pairs_y, PAIR, depth, LANES), BF16),
        in_specs=[SMEM, SMEM, VMEM, VMEM, VMEM, VMEM],
        out_specs=VMEM,
        name="pack",
    )(zone.reshape(1), lax.axis_index("yi").reshape(1), tokens.T, grad_out.T, expert_ids.T, probs.T)
    stacked = pl.pallas_call(
        weights_kernel,
        out_shape=jax.ShapeDtypeStruct((3 * hidden, wide), BF16),
        in_specs=[VMEM] * 3,
        out_specs=VMEM,
        name="widen_weights",
    )(w_gate[0].T, w_up[0].T, w_down[0])
    sent = packed.reshape(PAIR * pairs_y * PAIR, depth, LANES)
    quarter = lax.all_to_all(sent, ("zi",) + EP, split_axis=0, concat_axis=0, tiled=True)
    quarter, stacked = lax.optimization_barrier((quarter, stacked))
    weights = lax.all_gather(stacked, GROUP)
    along_z = lax.all_gather(quarter, "zo").reshape(chips_z, pairs_y * PAIR, depth, LANES)
    blocks = []
    for steps in range(chips_x):
        along = [(i, (i + steps) % chips_x) for i in range(chips_x)]
        block = lax.ppermute(along_z, "x", along) if steps else along_z
        blocks += [block, swap(block, "core")]

    regrouped = pl.pallas_call(
        regroup_kernel,
        out_shape=jax.ShapeDtypeStruct((3, groups * hidden, wide), BF16),
        in_specs=[VMEM],
        out_specs=VMEM,
        compiler_params=room(4),
        cost_estimate=pl.CostEstimate(flops=0, bytes_accessed=2 * 3 * groups * hidden * wide * 2, transcendentals=0),
        name="regroup",
    )(weights)
    sent_blocks = (3 * (features // LANES) + 1) * hidden // 16
    parts = pl.pallas_call(
        functools.partial(grads_kernel, features, hidden),
        out_shape=jax.ShapeDtypeStruct((groups, sent_blocks, 16, LANES), BF16),
        in_specs=[SMEM] * 3 + [VMEM] * (len(blocks) + 1),
        out_specs=VMEM,
        scratch_shapes=[pltpu.VMEM((chips_z, chips_x * CORES, depth, pairs_y * LANES), BF16)] * 2,
        compiler_params=room(20),
        name="grads",
    )(*(lax.axis_index(axis).reshape(1) for axis in ("core", "x", "yo")), *blocks, regrouped)
    met = lax.all_to_all(parts, GROUP, split_axis=0, concat_axis=0, tiled=True)
    grad_gate, grad_up, grad_down = pl.pallas_call(
        total_kernel,
        out_shape=[jax.ShapeDtypeStruct((units, features), BF16)] * 3,
        in_specs=[VMEM],
        out_specs=[VMEM] * 3,
        compiler_params=room(8),
        name="total",
    )(met)
    return grad_gate.T[None], grad_up.T[None], grad_down[None]


def solution(mesh, chips_x=CHIPS_X):
    section, ep = mesh.devices.shape
    shape = (section // (chips_x * CORES * PAIR), PAIR, chips_x, CORES, ep // PAIR, PAIR)
    fine = Mesh(mesh.devices.reshape(shape), SEC + EP)
    placed = (
        P(EP, SEC),
        P(EP, SEC),
        P(EP, None),
        P(EP, None),
        P(EP, None, SEC),
        P(EP, None, SEC),
        P(EP, SEC, None),
    )
    return jax.shard_map(
        shards,
        mesh=fine,
        in_specs=placed,
        out_specs=(P(EP, None, SEC), P(EP, None, SEC), P(EP, SEC, None)),
        check_vma=False,
    )
```

```python
import functools

import jax
import jax.numpy as jnp
from jax import lax
from jax.experimental import pallas as pl
from jax.experimental.pallas import tpu as pltpu
from jax.sharding import Mesh, PartitionSpec as P

BF16, F32 = jnp.bfloat16, jnp.float32
CORES = 2
CHIPS_X = 4
PAIR = 2
LANES = 128
SEC = ("zo", "zi", "x", "core")
EP = ("yo", "yi")
GROUP = ("zi", "yi")


def dot(a, b):
    return jnp.dot(a, b, preferred_element_type=F32)


def dot_t(a, b):
    return lax.dot_general(a, b, (((1,), (1,)), ((), ())), preferred_element_type=F32)


def spread(narrow_lane, wide_lane):
    return (narrow_lane == wide_lane - (wide_lane >> 4)) & ((wide_lane & 15) != 15)


def widen(rows, wide):
    narrow = rows.shape[1]
    pieces = []
    for start in range(0, wide, LANES):
        low = start - start // 16
        low = low // LANES * LANES
        high = min(narrow, low + 2 * LANES)
        source = lax.broadcasted_iota(jnp.int32, (high - low, LANES), 0) + low
        target = lax.broadcasted_iota(jnp.int32, (high - low, LANES), 1) + start
        chosen = spread(source, target).astype(F32).astype(BF16)
        pieces.append(dot(rows[:, low:high], chosen).astype(BF16))
    return jnp.concatenate(pieces, axis=1)


def narrowed(rows, narrow):
    wide = rows.shape[1]
    pieces = []
    for start in range(0, narrow, LANES):
        width = min(LANES, narrow - start)
        low = start // 15 * 16 // LANES * LANES
        last = start + width - 1
        high = min(wide, -(-(last // 15 * 16 + last % 15 + 1) // LANES) * LANES)
        source = lax.broadcasted_iota(jnp.int32, (high - low, width), 0) + low
        target = lax.broadcasted_iota(jnp.int32, (high - low, width), 1) + start
        chosen = spread(target, source).astype(F32).astype(BF16)
        pieces.append(dot(rows[:, low:high], chosen).astype(BF16))
    return jnp.concatenate(pieces, axis=1)


def half_turn(tile):
    return pltpu.roll(tile, LANES // 2, 1)


def turned(rows):
    tiles = [half_turn(rows[:, k : k + LANES]) for k in range(0, rows.shape[1], LANES)]
    return jnp.concatenate(tiles, axis=1)


def pack_kernel(zone, yi, *refs):
    sources, out, held, sems = refs[:4], refs[4], refs[5:9], refs[9]
    copies = [pltpu.make_async_copy(a, b, sems.at[k]) for k, (a, b) in enumerate(zip(sources, held))]
    for copy in copies:
        copy.start()
    for copy in copies:
        copy.wait()
    tokens, cotangent, ids, probs = held
    count = tokens.shape[1]
    mine = ids[...] == zone[0]
    weight = jnp.sum(jnp.where(mine, probs[...], 0.0), axis=0, keepdims=True)
    high = weight.astype(BF16).astype(F32)
    left = jnp.concatenate([tokens[...].astype(F32), high], axis=0)
    right = jnp.concatenate([cotangent[...].astype(F32), weight - high], axis=0)
    odd = yi[0] == 1
    first, second = jnp.where(odd, right, left), jnp.where(odd, left, right)
    lower = lax.broadcasted_iota(jnp.int32, (first.shape[0], LANES), 1) < LANES // 2
    for tile in range(count // LANES):
        a, b = first[:, tile * LANES : (tile + 1) * LANES], second[:, tile * LANES : (tile + 1) * LANES]
        quarters = (jnp.where(lower, a, half_turn(b)), jnp.where(lower, half_turn(a), b))
        for k, quarter in enumerate(quarters):
            zi, yi = divmod(2 * tile + k, PAIR)
            for yo in range(out.shape[1]):
                out[zi, yo, yi] = quarter.astype(BF16)


def weights_kernel(gate_w, up_w, down_w, out):
    hidden, wide = out.shape[0] // 3, out.shape[1]
    units = gate_w.shape[0]
    filler = jnp.zeros((hidden - units, gate_w.shape[1]), F32)
    rows = []
    for ref in (gate_w, up_w, down_w):
        rows += [ref[...].astype(F32), filler]
    out[...] = widen(jnp.concatenate(rows, axis=0).astype(BF16), wide)


def regroup_kernel(gathered, out):
    groups, stacked, wide = gathered.shape
    hidden = stacked // 3
    for k in range(3):
        out[k] = gathered[:, k * hidden : (k + 1) * hidden].reshape(groups * hidden, wide)


def grads_kernel(core_at, x_at, yo_at, *refs):
    blocks, (weights, out, inputs, cotangents) = refs[:-4], refs[-4:]
    chips_x = len(blocks) // CORES
    chips_z, tokens_y, depth, lanes = blocks[0].shape
    wide = weights.shape[2]
    groups, hidden = out.shape[0], out.shape[1] // 3
    core, x, yo = core_at[0], x_at[0], yo_at[0]
    lower = lax.broadcasted_iota(jnp.int32, (chips_z, depth, lanes), 2) < lanes // 2
    for k, ref in enumerate(blocks):
        steps, crossed = divmod(k, CORES)
        slot = lax.rem(x + chips_x - steps, chips_x) * CORES + (1 - core if crossed else core)
        for pair in range(tokens_y // 2):
            even, odd = ref[:, 2 * pair], ref[:, 2 * pair + 1]
            at = slice(pair * lanes, (pair + 1) * lanes)
            inputs[:, slot, :, at] = jnp.where(lower, even, odd)
            cotangents[:, slot, :, at] = jnp.where(lower, odd, even)
    total = tokens_y // 2 * lanes
    rows = inputs[...].reshape(wide, total)
    backs = cotangents[...].reshape(wide, total)

    units = groups * hidden
    both = dot(weights[:2].reshape(2 * units, wide), rows)
    gate, linear = both[:units], both[units:]
    back = turned(dot(weights[2], backs))
    shares = []
    for j in range(groups):
        expert = yo * PAIR + j % PAIR
        high = inputs[expert, 0].astype(F32)[depth - 1 : depth]
        low = turned(cotangents[expert, 0].astype(F32))[depth - 1 : depth]
        shares.append(jnp.broadcast_to(high + low, (hidden, total)))
    share = jnp.concatenate(shares, axis=0)
    back = back * share
    sigma = jax.nn.sigmoid(gate)
    lifted = turned(gate * sigma * linear * share).astype(BF16)
    gate_term = (back * linear * sigma * (1.0 + gate * (1.0 - sigma))).astype(BF16)
    linear_term = (back * gate * sigma).astype(BF16)
    upward = dot_t(jnp.concatenate([gate_term, linear_term], axis=0), rows).astype(BF16)
    grads = (upward[:units], upward[units:], dot_t(lifted, backs).astype(BF16))
    for k, grad in enumerate(grads):
        out[:, k * hidden : (k + 1) * hidden, :] = grad.reshape(groups, hidden, wide)


def total_kernel(parts, gate_g, up_g, down_g):
    hidden = parts.shape[1] // 3
    total = parts[0].astype(F32)
    for j in range(1, parts.shape[0]):
        total = total + parts[j].astype(F32)
    units, narrow = gate_g.shape
    slim = narrowed(total.astype(BF16), narrow).astype(F32)
    for k, ref in enumerate((gate_g, up_g, down_g)):
        ref[...] = slim[k * hidden : k * hidden + units].astype(BF16)


VMEM = pl.BlockSpec(memory_space=pltpu.VMEM)
SMEM = pl.BlockSpec(memory_space=pltpu.SMEM)


def room(mib):
    return pltpu.CompilerParams(vmem_limit_bytes=mib * 1024 * 1024)


def swap(value, axis):
    return lax.ppermute(value, axis, [(0, 1), (1, 0)])


def shards(tokens, grad_out, expert_ids, probs, w_gate, w_up, w_down):
    pairs_z, chips_x, pairs_y = lax.axis_size("zo"), lax.axis_size("x"), lax.axis_size("yo")
    chips_z, groups = pairs_z * PAIR, PAIR * PAIR
    count, width = tokens.shape
    features, units = w_gate.shape[1:]
    depth = width + 1
    wide = chips_z * chips_x * CORES * depth
    hidden = -(-units // 16) * 16
    zone = lax.axis_index(("zo", "zi"))

    sources = (tokens.T, grad_out.T, expert_ids.T, probs.T)
    packed = pl.pallas_call(
        pack_kernel,
        out_shape=jax.ShapeDtypeStruct((PAIR, pairs_y, PAIR, depth, LANES), BF16),
        in_specs=[SMEM] * 2 + [pl.BlockSpec(memory_space=pl.ANY)] * 4,
        out_specs=VMEM,
        scratch_shapes=[pltpu.VMEM(source.shape, source.dtype) for source in sources] + [pltpu.SemaphoreType.DMA((4,))],
        name="pack",
    )(zone.reshape(1), lax.axis_index("yi").reshape(1), *sources)
    stacked = pl.pallas_call(
        weights_kernel,
        out_shape=jax.ShapeDtypeStruct((3 * hidden, wide), BF16),
        in_specs=[VMEM] * 3,
        out_specs=VMEM,
        name="widen_weights",
    )(w_gate[0].T, w_up[0].T, w_down[0])
    sent = packed.reshape(PAIR * pairs_y * PAIR, depth, LANES)
    quarter = lax.all_to_all(sent, ("zi",) + EP, split_axis=0, concat_axis=0, tiled=True)
    quarter, stacked = lax.optimization_barrier((quarter, stacked))
    weights = lax.all_gather(stacked, GROUP)
    along_z = lax.all_gather(quarter, "zo").reshape(chips_z, pairs_y * PAIR, depth, LANES)
    blocks = []
    for steps in range(chips_x):
        along = [(i, (i + steps) % chips_x) for i in range(chips_x)]
        block = lax.ppermute(along_z, "x", along) if steps else along_z
        blocks += [block, swap(block, "core")]

    regrouped = pl.pallas_call(
        regroup_kernel,
        out_shape=jax.ShapeDtypeStruct((3, groups * hidden, wide), BF16),
        in_specs=[VMEM],
        out_specs=VMEM,
        compiler_params=room(4),
        cost_estimate=pl.CostEstimate(flops=0, bytes_accessed=2 * 3 * groups * hidden * wide * 2, transcendentals=0),
        name="regroup",
    )(weights)
    parts = pl.pallas_call(
        grads_kernel,
        out_shape=jax.ShapeDtypeStruct((groups, 3 * hidden, wide), BF16),
        in_specs=[SMEM] * 3 + [VMEM] * (len(blocks) + 1),
        out_specs=VMEM,
        scratch_shapes=[pltpu.VMEM((chips_z, chips_x * CORES, depth, pairs_y * LANES), BF16)] * 2,
        compiler_params=room(20),
        name="grads",
    )(*(lax.axis_index(axis).reshape(1) for axis in ("core", "x", "yo")), *blocks, regrouped)
    met = lax.all_to_all(parts, GROUP, split_axis=0, concat_axis=0, tiled=True)
    grad_gate, grad_up, grad_down = pl.pallas_call(
        total_kernel,
        out_shape=[jax.ShapeDtypeStruct((units, features), BF16)] * 3,
        in_specs=[VMEM],
        out_specs=[VMEM] * 3,
        compiler_params=room(8),
        name="total",
    )(met)
    return grad_gate.T[None], grad_up.T[None], grad_down[None]


def solution(mesh, chips_x=CHIPS_X):
    section, ep = mesh.devices.shape
    shape = (section // (chips_x * CORES * PAIR), PAIR, chips_x, CORES, ep // PAIR, PAIR)
    fine = Mesh(mesh.devices.reshape(shape), SEC + EP)
    placed = (
        P(EP, SEC),
        P(EP, SEC),
        P(EP, None),
        P(EP, None),
        P(EP, None, SEC),
        P(EP, None, SEC),
        P(EP, SEC, None),
    )
    return jax.shard_map(
        shards,
        mesh=fine,
        in_specs=placed,
        out_specs=(P(EP, None, SEC), P(EP, None, SEC), P(EP, SEC, None)),
        check_vma=False,
    )
```

```python
import functools

import jax
import jax.numpy as jnp
from jax import lax
from jax.experimental import pallas as pl
from jax.experimental.pallas import tpu as pltpu
from jax.sharding import Mesh, PartitionSpec as P

BF16, F32 = jnp.bfloat16, jnp.float32
CORES = 2
CHIPS_X = 4
PAIR = 2
LANES = 128
SEC = ("zo", "zi", "x", "core")
EP = ("yo", "yi")
GROUP = ("zi", "yi")


def dot(a, b):
    return jnp.dot(a, b, preferred_element_type=F32)


def dot_t(a, b):
    return lax.dot_general(a, b, (((1,), (1,)), ((), ())), preferred_element_type=F32)


def spread(narrow_lane, wide_lane):
    return (narrow_lane == wide_lane - (wide_lane >> 4)) & ((wide_lane & 15) != 15)


def widen(rows, wide):
    narrow = rows.shape[1]
    pieces = []
    for start in range(0, wide, LANES):
        low = start - start // 16
        low = low // LANES * LANES
        high = min(narrow, low + 2 * LANES)
        source = lax.broadcasted_iota(jnp.int32, (high - low, LANES), 0) + low
        target = lax.broadcasted_iota(jnp.int32, (high - low, LANES), 1) + start
        chosen = spread(source, target).astype(F32).astype(BF16)
        pieces.append(dot(rows[:, low:high], chosen).astype(BF16))
    return jnp.concatenate(pieces, axis=1)


def narrowed(rows, narrow):
    wide = rows.shape[1]
    pieces = []
    for start in range(0, narrow, LANES):
        width = min(LANES, narrow - start)
        low = start // 15 * 16 // LANES * LANES
        last = start + width - 1
        high = min(wide, -(-(last // 15 * 16 + last % 15 + 1) // LANES) * LANES)
        source = lax.broadcasted_iota(jnp.int32, (high - low, width), 0) + low
        target = lax.broadcasted_iota(jnp.int32, (high - low, width), 1) + start
        chosen = spread(target, source).astype(F32).astype(BF16)
        pieces.append(dot(rows[:, low:high], chosen).astype(BF16))
    return jnp.concatenate(pieces, axis=1)


def half_turn(tile):
    return pltpu.roll(tile, LANES // 2, 1)


def turned(rows):
    tiles = [half_turn(rows[:, k : k + LANES]) for k in range(0, rows.shape[1], LANES)]
    return jnp.concatenate(tiles, axis=1)


def pack_kernel(zone, yi, tokens, cotangent, ids, probs, out):
    count = tokens.shape[1]
    mine = ids[...] == zone[0]
    weight = jnp.sum(jnp.where(mine, probs[...], 0.0), axis=0, keepdims=True)
    high = weight.astype(BF16).astype(F32)
    left = jnp.concatenate([tokens[...].astype(F32), high], axis=0)
    right = jnp.concatenate([cotangent[...].astype(F32), weight - high], axis=0)
    odd = yi[0] == 1
    first, second = jnp.where(odd, right, left), jnp.where(odd, left, right)
    lower = lax.broadcasted_iota(jnp.int32, (first.shape[0], LANES), 1) < LANES // 2
    for tile in range(count // LANES):
        a, b = first[:, tile * LANES : (tile + 1) * LANES], second[:, tile * LANES : (tile + 1) * LANES]
        quarters = (jnp.where(lower, a, half_turn(b)), jnp.where(lower, half_turn(a), b))
        for k, quarter in enumerate(quarters):
            zi, yi = divmod(2 * tile + k, PAIR)
            for yo in range(out.shape[1]):
                out[zi, yo, yi] = quarter.astype(BF16)


def weights_kernel(gate_w, up_w, down_w, out):
    hidden, wide = out.shape[0] // 3, out.shape[1]
    units = gate_w.shape[0]
    filler = jnp.zeros((hidden - units, gate_w.shape[1]), F32)
    rows = []
    for ref in (gate_w, up_w, down_w):
        rows += [ref[...].astype(F32), filler]
    out[...] = widen(jnp.concatenate(rows, axis=0).astype(BF16), wide)


def regroup_kernel(gathered, out):
    groups, stacked, wide = gathered.shape
    hidden = stacked // 3
    for k in range(3):
        out[k] = gathered[:, k * hidden : (k + 1) * hidden].reshape(groups * hidden, wide)


def grads_kernel(core_at, x_at, yo_at, *refs):
    blocks, (weights, out, down, inputs, cotangents) = refs[:-5], refs[-5:]
    chips_x = len(blocks) // CORES
    chips_z, tokens_y, depth, lanes = blocks[0].shape
    wide = weights.shape[2]
    groups, hidden = down.shape[0], down.shape[1]
    core, x, yo = core_at[0], x_at[0], yo_at[0]
    lower = lax.broadcasted_iota(jnp.int32, (chips_z, depth, lanes), 2) < lanes // 2
    for k, ref in enumerate(blocks):
        steps, crossed = divmod(k, CORES)
        slot = lax.rem(x + chips_x - steps, chips_x) * CORES + (1 - core if crossed else core)
        for pair in range(tokens_y // 2):
            even, odd = ref[:, 2 * pair], ref[:, 2 * pair + 1]
            at = slice(pair * lanes, (pair + 1) * lanes)
            inputs[:, slot, :, at] = jnp.where(lower, even, odd)
            cotangents[:, slot, :, at] = jnp.where(lower, odd, even)
    total = tokens_y // 2 * lanes
    rows = inputs[...].reshape(wide, total)
    backs = cotangents[...].reshape(wide, total)

    units = groups * hidden
    both = dot(weights[:2].reshape(2 * units, wide), rows)
    gate, linear = both[:units], both[units:]
    back = turned(dot(weights[2], backs))
    shares = []
    for j in range(groups):
        expert = yo * PAIR + j % PAIR
        high = inputs[expert, 0].astype(F32)[depth - 1 : depth]
        low = turned(cotangents[expert, 0].astype(F32))[depth - 1 : depth]
        shares.append(jnp.broadcast_to(high + low, (hidden, total)))
    share = jnp.concatenate(shares, axis=0)
    back = back * share
    sigma = jax.nn.sigmoid(gate)
    lifted = turned(gate * sigma * linear * share).astype(BF16)
    gate_term = (back * linear * sigma * (1.0 + gate * (1.0 - sigma))).astype(BF16)
    linear_term = (back * gate * sigma).astype(BF16)
    upward = dot_t(jnp.concatenate([gate_term, linear_term], axis=0), rows).astype(BF16)
    grads = (upward[:units], upward[units:], dot_t(lifted, backs).astype(BF16))
    for k, grad in enumerate(grads):
        target = down if k == 2 else out
        target[:, k % 2 * hidden : (k % 2 + 1) * hidden, :] = grad.reshape(groups, hidden, wide)


def total_kernel(first, second, gate_g, up_g, down_g):
    hidden = second.shape[1]
    totals = []
    for parts in (first, second):
        total = parts[0].astype(F32)
        for j in range(1, parts.shape[0]):
            total = total + parts[j].astype(F32)
        totals.append(total)
    total = jnp.concatenate(totals, axis=0)
    units, narrow = gate_g.shape
    slim = narrowed(total.astype(BF16), narrow).astype(F32)
    for k, ref in enumerate((gate_g, up_g, down_g)):
        ref[...] = slim[k * hidden : k * hidden + units].astype(BF16)


VMEM = pl.BlockSpec(memory_space=pltpu.VMEM)
SMEM = pl.BlockSpec(memory_space=pltpu.SMEM)


def room(mib):
    return pltpu.CompilerParams(vmem_limit_bytes=mib * 1024 * 1024)


def swap(value, axis):
    return lax.ppermute(value, axis, [(0, 1), (1, 0)])


def shards(tokens, grad_out, expert_ids, probs, w_gate, w_up, w_down):
    pairs_z, chips_x, pairs_y = lax.axis_size("zo"), lax.axis_size("x"), lax.axis_size("yo")
    chips_z, groups = pairs_z * PAIR, PAIR * PAIR
    count, width = tokens.shape
    features, units = w_gate.shape[1:]
    depth = width + 1
    wide = chips_z * chips_x * CORES * depth
    hidden = -(-units // 16) * 16
    zone = lax.axis_index(("zo", "zi"))

    packed = pl.pallas_call(
        pack_kernel,
        out_shape=jax.ShapeDtypeStruct((PAIR, pairs_y, PAIR, depth, LANES), BF16),
        in_specs=[SMEM, SMEM, VMEM, VMEM, VMEM, VMEM],
        out_specs=VMEM,
        name="pack",
    )(zone.reshape(1), lax.axis_index("yi").reshape(1), tokens.T, grad_out.T, expert_ids.T, probs.T)
    stacked = pl.pallas_call(
        weights_kernel,
        out_shape=jax.ShapeDtypeStruct((3 * hidden, wide), BF16),
        in_specs=[VMEM] * 3,
        out_specs=VMEM,
        name="widen_weights",
    )(w_gate[0].T, w_up[0].T, w_down[0])
    sent = packed.reshape(PAIR * pairs_y * PAIR, depth, LANES)
    quarter = lax.all_to_all(sent, ("zi",) + EP, split_axis=0, concat_axis=0, tiled=True)
    quarter, stacked = lax.optimization_barrier((quarter, stacked))
    weights = lax.all_gather(stacked, GROUP)
    along_z = lax.all_gather(quarter, "zo").reshape(chips_z, pairs_y * PAIR, depth, LANES)
    blocks = []
    for steps in range(chips_x):
        along = [(i, (i + steps) % chips_x) for i in range(chips_x)]
        block = lax.ppermute(along_z, "x", along) if steps else along_z
        blocks += [block, swap(block, "core")]

    regrouped = pl.pallas_call(
        regroup_kernel,
        out_shape=jax.ShapeDtypeStruct((3, groups * hidden, wide), BF16),
        in_specs=[VMEM],
        out_specs=VMEM,
        compiler_params=room(4),
        cost_estimate=pl.CostEstimate(flops=0, bytes_accessed=2 * 3 * groups * hidden * wide * 2, transcendentals=0),
        name="regroup",
    )(weights)
    parts = pl.pallas_call(
        grads_kernel,
        out_shape=[jax.ShapeDtypeStruct((groups, k * hidden, wide), BF16) for k in (2, 1)],
        in_specs=[SMEM] * 3 + [VMEM] * (len(blocks) + 1),
        out_specs=[VMEM] * 2,
        scratch_shapes=[pltpu.VMEM((chips_z, chips_x * CORES, depth, pairs_y * LANES), BF16)] * 2,
        compiler_params=room(20),
        name="grads",
    )(*(lax.axis_index(axis).reshape(1) for axis in ("core", "x", "yo")), *blocks, regrouped)
    met = [lax.all_to_all(part, GROUP, split_axis=0, concat_axis=0, tiled=True) for part in parts]
    grad_gate, grad_up, grad_down = pl.pallas_call(
        total_kernel,
        out_shape=[jax.ShapeDtypeStruct((units, features), BF16)] * 3,
        in_specs=[VMEM] * 2,
        out_specs=[VMEM] * 3,
        compiler_params=room(8),
        name="total",
    )(*met)
    return grad_gate.T[None], grad_up.T[None], grad_down[None]


def solution(mesh, chips_x=CHIPS_X):
    section, ep = mesh.devices.shape
    shape = (section // (chips_x * CORES * PAIR), PAIR, chips_x, CORES, ep // PAIR, PAIR)
    fine = Mesh(mesh.devices.reshape(shape), SEC + EP)
    placed = (
        P(EP, SEC),
        P(EP, SEC),
        P(EP, None),
        P(EP, None),
        P(EP, None, SEC),
        P(EP, None, SEC),
        P(EP, SEC, None),
    )
    return jax.shard_map(
        shards,
        mesh=fine,
        in_specs=placed,
        out_specs=(P(EP, None, SEC), P(EP, None, SEC), P(EP, SEC, None)),
        check_vma=False,
    )
```
